128 devices in a mesh: proj: 32 (over z, x, core), det: 4 (over y).
Axes of the slice: x: 4, y: 4, z: 4, core: 2. Of those that a mesh axis runs over, the one named last changes fastest.
Arguments:
- raw_frames: bfloat16 [2048, 64, 2048], P('proj', None, 'det'), may hold values from 0.25 to 2.125
- slot_angle: int32 [2048], replicated, may hold values from 0 to 1024, as said below
- segment_of: int32 [1024], replicated, may hold values from 0 to 7, never falling along the last dimension, each value on 1 to 256 neighbouring positions
- seg_owner: int32 [8], replicated, may hold values from 0 to 31
- flat_stack: float32 [256, 64, 2048], P('proj', None, 'det'), may hold values from 1 to 2
- dark_stack: float32 [256, 64, 2048], P('proj', None, 'det'), may hold values from 0 to 0.2
- row_order: int32 [64], replicated, may hold values from 0 to 63, each once
- bin_counts: int32 [64], replicated, may hold values from 2 to 5
Outputs:
- codes: float32 [1024, 64, 2048], P(None, 'proj', 'det')
The draws below stay inside these ranges and needn't reach their ends.
Inputs may be any that keep to these rules, and one draw needn't show every extreme that they name: `slot_angle`: index p of proj holds slots 64 * p to 64 * p + 63. Every angle 0 to 1023 stands in exactly one slot; a device's filled slots come first and its other slots hold 1024. Indices 2k and 2k + 1 of proj together fill exactly 64 slots, and some index fills all 64. `segment_of`: never falls from one angle to the next; every segment has an angle. `seg_owner`: each value is an index of proj. `row_order`: A permutation of the rows.
All inputs are finite; a program needn't handle non-finite values.
Results may differ from the reference program's by a relative error of at most 0.0029.
Values may be sent and summed in bfloat16 or wider, within the bound.
A program may use at most 128 MiB of HBM per device.

```python
import math
import jax
import jax.numpy as jnp
import numpy as np

ANG_DEV = 32
SLOTS = 64
ANGLES = 1024
SLOTS_ALL = 2048
ROWS = 64
COLS = 2048
SEGS = 8
STACK = 256
RIM = 8


def draw_raw_frames(key, part):
    key = jax.random.fold_in(key, 5)
    key_gain, key_level, key_slot = jax.random.split(key, 3)
    gain = jnp.exp(jax.random.uniform(key_gain, (ROWS, COLS), jnp.float32, math.log(0.8), math.log(1.25)))
    column = jnp.arange(COLS, dtype=jnp.float32) / (COLS - 1)
    spread = jax.random.uniform(key_slot, (SLOTS_ALL, 1, 1), jnp.float32, 0.0, 1.0)
    slot_factor = jnp.exp(math.log(0.1) * spread)
    level = jax.random.uniform(key_level, (SLOTS_ALL, ROWS, COLS), jnp.float32, 0.2, 1.0) * slot_factor
    thickness = 3.0 * (1.0 - column)
    values = 0.25 + 1.5 * jnp.exp(-thickness)[None, None, :] * level * gain[None]
    return values.astype(jnp.bfloat16)


def draw_flat_stack(key, part):
    key = jax.random.fold_in(key, 17)
    values = jax.random.uniform(key, (STACK, ROWS, COLS), jnp.float32, 1.0, 2.0)
    return values


def draw_dark_stack(key, part):
    key = jax.random.fold_in(key, 23)
    values = jax.random.uniform(key, (STACK, ROWS, COLS), jnp.float32, 0.0, 0.2)
    return values


def draw_slot_angle(key, part):
    key = jax.random.fold_in(key, 11)
    key_extra, key_forced, key_flip, key_perm = jax.random.split(key, 4)
    devices = ANGLES // ANG_DEV
    pairs = devices // 2
    extra = jax.random.randint(key_extra, (pairs,), 0, ANG_DEV + 1)
    forced = jax.random.randint(key_forced, (), 0, pairs)
    extra = jnp.where(jnp.arange(pairs) == forced, ANG_DEV, extra)
    flipped = jax.random.randint(key_flip, (pairs,), 0, 2)
    even_count = ANG_DEV + jnp.where(flipped == 0, extra, -extra)
    odd_count = 2 * ANG_DEV - even_count
    counts = jnp.stack([even_count, odd_count], axis=1).reshape(devices)
    offsets = jnp.cumsum(counts) - counts
    shuffled = jax.random.permutation(key_perm, ANGLES)
    within = jnp.arange(SLOTS)
    index = offsets[:, None] + within[None, :]
    filled = within[None, :] < counts[:, None]
    values = jnp.where(filled, shuffled[jnp.clip(index, 0, ANGLES - 1)], ANGLES)
    return values.reshape(devices * SLOTS).astype(jnp.int32)


def plant(entries, key, least, high):
    longest = entries.shape.index(max(entries.shape))
    spots = []
    for shift in (0, 1):
        where = [jax.random.randint(jax.random.fold_in(key, axis), (), 0, length) for axis, length in enumerate(entries.shape)]
        where[longest] = (where[longest] + shift) % entries.shape[longest]
        spots.append(tuple(where))
    return entries.at[spots[0]].set(least).at[spots[1]].set(high)


def split_up(count, total, limit, skew):
    weights = [(1 << 20) // math.isqrt(rank ** skew) + 1 for rank in range(2, count + 1)]
    rest, given = total - limit - (count - 1), [1] * (count - 1)
    while rest > 0:
        free = [i for i in range(count - 1) if given[i] < limit]
        mass, budget = sum([weights[i] for i in free]), rest
        for i in free:
            more = min(limit - given[i], max(1, budget * weights[i] // mass), rest)
            given[i] = given[i] + more
            rest = rest - more
    return np.array([limit] + given)


def ragged(rng, count, total, most, slope):
    if count == 2:
        one = jax.random.randint(rng, (), max(1, total - most), min(most, total - 1) + 1)
        return jnp.stack([one, total - one])
    tallies = jnp.asarray(split_up(count, total, most, slope), jnp.int32)
    pairs = (count - 1) // 2
    source_of, sink = tallies[1:1 + 2 * pairs:2], tallies[2:2 + 2 * pairs:2]
    margin = jnp.minimum(source_of - 1, most - sink)
    moved = jax.random.randint(jax.random.fold_in(rng, 1), (pairs,), 0, 1 << 20) % (margin + 1)
    tallies = tallies.at[1:1 + 2 * pairs:2].set(source_of - moved).at[2:2 + 2 * pairs:2].set(sink + moved)
    return tallies[jax.random.permutation(jax.random.fold_in(rng, 2), count)]


def setup_inputs(seed: int = 0) -> dict:
    key_of = jax.random.split(jax.random.key(seed), 9)
    return {
        "raw_frames": draw_raw_frames(jax.random.fold_in(key_of[8], 71), 0),
        "slot_angle": draw_slot_angle(jax.random.fold_in(key_of[8], 71), 0),
        "segment_of": jnp.searchsorted(jnp.cumsum(ragged(key_of[2], SEGS, ANGLES, 2 * ANGLES // SEGS, 0)), jnp.arange(ANGLES), side="right").astype(jnp.int32),
        "seg_owner": plant(jax.random.randint(key_of[3], (SEGS,), 0, ANGLES // ANG_DEV), jax.random.fold_in(key_of[3], 1), 0, (ANGLES // ANG_DEV) - 1).astype(jnp.int32),
        "flat_stack": draw_flat_stack(jax.random.fold_in(key_of[8], 71), 0),
        "dark_stack": draw_dark_stack(jax.random.fold_in(key_of[8], 71), 0),
        "row_order": jax.random.permutation(key_of[6], ROWS).astype(jnp.int32),
        "bin_counts": plant(jax.random.randint(key_of[7], (ROWS,), 2, 6), jax.random.fold_in(key_of[7], 1), 2, 5).astype(jnp.int32),
    }


def reference(raw_frames, slot_angle, segment_of, seg_owner, flat_stack, dark_stack, row_order, bin_counts):
    total_angles = segment_of.shape[0]
    segments = seg_owner.shape[0]
    columns = raw_frames.shape[2]
    locate = jnp.zeros((total_angles,), jnp.int32).at[slot_angle].set(
        jnp.arange(slot_angle.shape[0], dtype=jnp.int32), mode="drop")
    frames = raw_frames[locate]
    field_index = (seg_owner * segments + jnp.arange(segments, dtype=jnp.int32)).astype(jnp.int32)
    flat_field = flat_stack[field_index]
    dark_field = dark_stack[field_index]
    flat_rows = flat_field[segment_of]
    dark_rows = dark_field[segment_of]
    ratio = (frames.astype(jnp.float32) - dark_rows) / (flat_rows - dark_rows)
    sinogram = (-jnp.log(ratio)).astype(jnp.bfloat16)
    sinogram = sinogram[:, row_order, :]
    profile = jnp.sum(sinogram, axis=0, dtype=jnp.float32) / total_angles
    padded = jnp.pad(profile, ((0, 0), (RIM, RIM)))
    window_sum = padded[:, 0:columns]
    for offset in range(1, 2 * RIM + 1):
        window_sum = window_sum + padded[:, offset:offset + columns]
    column = jnp.arange(columns, dtype=jnp.int32)
    counted = (jnp.minimum(column + RIM, columns - 1) - jnp.maximum(column - RIM, 0) + 1).astype(jnp.float32)
    smooth = window_sum / counted
    corrected = sinogram.astype(jnp.float32) - (profile - smooth)[None]
    scale = jnp.sum(jnp.abs(corrected), axis=(0, 2)) / (total_angles * columns) + 1e-6
    factor = bin_counts[row_order].astype(jnp.float32) / scale
    return corrected * factor[None, :, None]
```

```python
import functools

import jax
import jax.numpy as jnp
from jax import lax
from jax.experimental import pallas as pl
from jax.experimental.pallas import tpu as pltpu
from jax.sharding import PartitionSpec as P

MESH = pl.DeviceIdType.MESH

SLOTS = 64
HALF = 32
ANGLES = 1024
ROWS = 64
COLS_DEV = 512
COLS = 2048
SEGS = 8
RIM = 8
PROJ = 32
CHIPS = 16
DET = 4
TILES = COLS_DEV // 128
PARTS = 4
FRAMES = HALF // PARTS
PAIRS = FRAMES // 2
EPSILON = 1e-6
DARK_STEP = 0.2 / 65535.0
FLAT_STEP = 1.0 / 65535.0


def stack_tiles(frame):
    return jnp.concatenate([frame[:, 128 * t : 128 * (t + 1)] for t in range(TILES)], axis=0)


def coded(field, low, step):
    q = jnp.floor((field - low) * (1.0 / step) + 0.5)
    q = jnp.clip(q, 0.0, 65535.0)
    high = jnp.floor(q * (1.0 / 256.0))
    return high.astype(jnp.bfloat16), (q - 256.0 * high).astype(jnp.bfloat16)


def exchange(
    slot_angle,
    segment_of,
    seg_owner,
    row_order,
    bin_counts,
    raw,
    flat,
    dark,
    y_out,
    delta_out,
    factor_out,
    where_out,
    own,
    other,
    send,
    recv,
    flat_v,
    dark_v,
    pick_f,
    pick,
    fsend,
    fpart,
    fjoin,
    frecv,
    dark_s,
    logflat_s,
    profs,
    sums,
    load_sem,
    field_sem,
    swap_ssem,
    swap_rsem,
    send_sem,
    recv_sem,
    fswap_sem,
    fsend_sem,
    frecv_sem,
    small_ssem,
    small_rsem,
):
    proj = lax.axis_index("proj")
    det = lax.axis_index("det")
    core = proj % 2
    chip = proj // 2
    col = chip % 4
    lay = chip // 4
    mate = proj + 1 - 2 * core

    def away(t):
        c = (core + t) % 2
        x = (col + t // 2) % 4
        z = (lay + t // 8) % 4
        return (z * 4 + x) * 2 + c

    def back(t):
        c = (core + t) % 2
        x = (col + 4 - (t // 2) % 4) % 4
        z = (lay + 4 - t // 8) % 4
        return (z * 4 + x) * 2 + c

    loads = []
    for part in range(PARTS):
        copy = pltpu.make_async_copy(
            raw.at[pl.ds(FRAMES * part, FRAMES)],
            own.at[pl.ds(FRAMES * part, FRAMES)],
            load_sem.at[part],
        )
        copy.start()
        loads.append(copy)
    flat_copy = pltpu.make_async_copy(flat, flat_v, field_sem.at[0])
    dark_copy = pltpu.make_async_copy(dark, dark_v, field_sem.at[1])
    flat_copy.start()
    dark_copy.start()

    barrier = pltpu.get_barrier_semaphore()

    @pl.loop(1, PROJ)
    def _(t):
        pl.semaphore_signal(
            barrier, inc=1, device_id=(away(t), det), device_id_type=MESH
        )

    for t in range(1, DET):
        pl.semaphore_signal(
            barrier, inc=1, device_id=(proj, (det + t) % DET), device_id_type=MESH
        )

    sub = lax.broadcasted_iota(jnp.int32, (8, 256), 0)
    lane = lax.broadcasted_iota(jnp.int32, (8, 256), 1)

    @pl.loop(0, PROJ)
    def _(i):
        p = 2 * (i % CHIPS) + i // CHIPS
        row = jnp.where(sub % 2 == 0, row_order[2 * p], row_order[2 * p + 1])
        hit = lane == row + (sub // 2) * ROWS
        pick_f[pl.ds(pl.multiple_of(8 * i, 8), 8), :] = jnp.where(hit, 1.0, 0.0)

    pick[...] = pick_f[...].astype(jnp.bfloat16)

    pl.semaphore_wait(barrier, PROJ - 1 + DET - 1)

    swaps = []
    for part in range(PARTS):
        first = HALF - FRAMES * (part + 1)
        copy = pltpu.make_async_remote_copy(
            src_ref=raw.at[pl.ds(HALF + first, FRAMES)],
            dst_ref=other.at[pl.ds(first, FRAMES)],
            send_sem=swap_ssem.at[part],
            recv_sem=swap_rsem.at[part],
            device_id=(mate, det),
            device_id_type=MESH,
        )
        copy.start()
        swaps.append(copy)

    def frame_copy(part, t, target, slot):
        return pltpu.make_async_remote_copy(
            src_ref=send.at[part, slot],
            dst_ref=recv.at[part, proj],
            send_sem=send_sem.at[part, t],
            recv_sem=recv_sem.at[part, proj],
            device_id=(target, det),
            device_id_type=MESH,
        )

    def slot_of(p):
        return (p % 2) * CHIPS + p // 2

    def ship_frames(part):
        loads[part].wait()
        swaps[part].wait_recv()

        @pl.loop(0, PAIRS)
        def _(j):
            merged = []
            for f in range(2):
                k = FRAMES * part + 2 * j + f
                filled = slot_angle[SLOTS * proj + k] < ANGLES
                merged.append(stack_tiles(jnp.where(filled, own[k], other[HALF - 1 - k])))
            moved = jnp.dot(
                pick[...], jnp.concatenate(merged, axis=1), preferred_element_type=jnp.float32
            ).reshape(PROJ, 8, 256)
            pair = jnp.concatenate([moved[:, :, :128], moved[:, :, 128:]], axis=1)
            send[part, :, j] = pair.astype(jnp.bfloat16)

        @pl.loop(1, PROJ)
        def _(t):
            target = away(t)
            frame_copy(part, t, target, slot_of(target)).start()

        recv[part, proj] = send[part, slot_of(proj)]

    def join_copy():
        return pltpu.make_async_remote_copy(
            src_ref=fsend.at[pl.ds((1 - core) * CHIPS, CHIPS)],
            dst_ref=fpart,
            send_sem=fswap_sem.at[0],
            recv_sem=fswap_sem.at[1],
            device_id=(mate, det),
            device_id_type=MESH,
        )

    def field_copy(t, target_chip):
        return pltpu.make_async_remote_copy(
            src_ref=fjoin.at[target_chip],
            dst_ref=frecv.at[chip],
            send_sem=fsend_sem.at[t],
            recv_sem=frecv_sem.at[chip],
            device_id=(2 * target_chip + core, det),
            device_id_type=MESH,
        )

    def code_fields():
        flat_copy.wait()
        dark_copy.wait()

        @pl.loop(0, SEGS)
        def _(s):
            mine = jnp.where(seg_owner[s] == proj, 1.0, 0.0)
            moved = []
            for ref, low, step in ((flat_v, 1.0, FLAT_STEP), (dark_v, 0.0, DARK_STEP)):
                high, small = coded(stack_tiles(ref[s]), low, step)
                both = jnp.dot(
                    pick[...], jnp.concatenate([high, small], axis=1), preferred_element_type=jnp.float32
                )
                code = (both[:, :128] * 256.0 + both[:, 128:] - 32768.0) * mine
                moved.append(code.reshape(PROJ, 8, 128))
            pair = jnp.concatenate(moved, axis=1)
            fsend[:, s] = pair.astype(jnp.int32).astype(jnp.int16)

        join_copy().start()

    def ship_fields():
        join_copy().wait()

        @pl.loop(0, CHIPS)
        def _(i):
            fjoin[i] = (
                fsend[core * CHIPS + i].astype(jnp.int32) + fpart[i].astype(jnp.int32)
            ).astype(jnp.int16)

        @pl.loop(1, CHIPS)
        def _(t):
            field_copy(t, away(2 * t) // 2).start()

        frecv[chip] = fjoin[chip]

    def take_fields():
        @pl.loop(1, CHIPS)
        def _(t):
            source = back(2 * t) // 2
            pltpu.make_async_remote_copy(
                src_ref=fjoin.at[source],
                dst_ref=frecv.at[source],
                send_sem=fsend_sem.at[t],
                recv_sem=frecv_sem.at[source],
                device_id=(2 * source + core, det),
                device_id_type=MESH,
            ).wait_recv()

        @pl.loop(0, SEGS)
        def _(s):
            total = frecv[0, s].astype(jnp.int32)
            for i in range(1, CHIPS):
                total = total + frecv[i, s].astype(jnp.int32)
            code = (total + 32768).astype(jnp.float32)
            f = 1.0 + code[:8] * FLAT_STEP
            d = code[8:] * DARK_STEP
            dark_s[s] = d
            logflat_s[s] = jnp.log(f - d)

    ship_frames(0)
    code_fields()
    ship_frames(1)
    ship_fields()
    ship_frames(2)
    ship_frames(3)
    take_fields()

    angle_id = (
        lax.broadcasted_iota(jnp.int32, (8, 128), 0) * 128
        + lax.broadcasted_iota(jnp.int32, (8, 128), 1)
    )

    def absorb(part, source, carry):
        acc0, acc1, places = carry
        accs = [acc0, acc1]
        for j in range(PAIRS):
            x = recv[part, source, j].astype(jnp.float32)
            for f in range(2):
                k = FRAMES * part + 2 * j + f
                here = slot_angle[SLOTS * source + k]
                pair = source + 1 - 2 * (source % 2)
                there = slot_angle[SLOTS * pair + SLOTS - 1 - k]
                angle = jnp.where(here < ANGLES, here, there)
                s = segment_of[angle]
                y = logflat_s[s] - jnp.log(x[8 * f : 8 * f + 8] - dark_s[s])
                y = y.astype(jnp.bfloat16).astype(jnp.float32)
                y_out[source * HALF + k] = y
                accs[f] = accs[f] + y
                places = jnp.where(angle_id == angle, source * HALF + k, places)
        return accs[0], accs[1], places

    zero = jnp.zeros((8, 128), jnp.float32)
    carry = (zero, zero, jnp.zeros((8, 128), jnp.int32))
    for part in range(PARTS):
        carry = absorb(part, proj, carry)

        def step(t, carry, part=part):
            source = back(t)
            pltpu.make_async_remote_copy(
                src_ref=send.at[part, 0],
                dst_ref=recv.at[part, source],
                send_sem=send_sem.at[part, t],
                recv_sem=recv_sem.at[part, source],
                device_id=(source, det),
                device_id_type=MESH,
            ).wait_recv()
            return absorb(part, source, carry)

        carry = lax.fori_loop(1, PROJ, step, carry)
    where_out[...] = carry[2]
    profile = (carry[0] + carry[1]) * (1.0 / ANGLES)

    def share(ref, which):
        copies = []
        for t in range(1, DET):
            copies.append(
                pltpu.make_async_remote_copy(
                    src_ref=ref.at[det],
                    dst_ref=ref.at[det],
                    send_sem=small_ssem.at[which, t],
                    recv_sem=small_rsem.at[which, det],
                    device_id=(proj, (det + t) % DET),
                    device_id_type=MESH,
                )
            )
            copies[-1].start()
        for t in range(1, DET):
            source = (det + t) % DET
            pltpu.make_async_remote_copy(
                src_ref=ref.at[source],
                dst_ref=ref.at[source],
                send_sem=small_ssem.at[which, t],
                recv_sem=small_rsem.at[which, source],
                device_id=(proj, source),
                device_id_type=MESH,
            ).wait_recv()
        return copies

    profs[det] = profile
    copies = share(profs, 0)
    sub = lax.broadcasted_iota(jnp.int32, (8, 128), 0)
    lane = lax.broadcasted_iota(jnp.int32, (8, 128), 1)
    before = profs[(det + DET - 1) % DET]
    after = profs[(det + 1) % DET]
    before = jnp.where(det > 0, before, jnp.zeros_like(before))
    after = jnp.where(det < DET - 1, after, jnp.zeros_like(after))
    low = jnp.where(sub < 2, pltpu.roll(before, 2, 0), pltpu.roll(profile, 2, 0))
    high = jnp.where(sub >= 6, pltpu.roll(after, 6, 0), pltpu.roll(profile, 6, 0))
    window = profile
    for o in range(1, RIM + 1):
        window = window + jnp.where(lane >= o, pltpu.roll(profile, o, 1), pltpu.roll(low, o, 1))
        window = window + jnp.where(
            lane < 128 - o, pltpu.roll(profile, 128 - o, 1), pltpu.roll(high, 128 - o, 1)
        )
    column = det * COLS_DEV + (sub // 2) * 128 + lane
    counted = jnp.minimum(column + RIM, COLS - 1) - jnp.maximum(column - RIM, 0) + 1
    delta = profile - window / counted.astype(jnp.float32)
    delta_out[...] = delta

    def magnitude(i, accs):
        return tuple(
            accs[u] + jnp.abs(y_out[i * 16 + u] - delta) + jnp.abs(y_out[i * 16 + 8 + u] - delta)
            for u in range(8)
        )

    accs = lax.fori_loop(0, ANGLES // 16, magnitude, (zero,) * 8)
    total = ((accs[0] + accs[1]) + (accs[2] + accs[3])) + ((accs[4] + accs[5]) + (accs[6] + accs[7]))
    sums[det] = total
    copies += share(sums, 1)
    total = (sums[0] + sums[1]) + (sums[2] + sums[3])
    rows = jnp.broadcast_to(jnp.sum(total, axis=1, keepdims=True), (8, 128))
    rows = rows + pltpu.roll(rows, 4, 0)
    rows = rows + pltpu.roll(rows, 2, 0)
    scale = rows * (1.0 / (ANGLES * COLS)) + EPSILON
    bins = jnp.where(
        sub % 2 == 0,
        bin_counts[row_order[2 * proj]],
        bin_counts[row_order[2 * proj + 1]],
    ).astype(jnp.float32)
    factor_out[...] = bins / scale

    for copy in copies:
        copy.wait_send()
    for copy in swaps:
        copy.wait_send()

    @pl.loop(1, CHIPS)
    def _(t):
        field_copy(t, away(2 * t) // 2).wait_send()

    for part in range(PARTS):

        @pl.loop(1, PROJ)
        def _(t, part=part):
            target = away(t)
            frame_copy(part, t, target, slot_of(target)).wait_send()


BLOCK = 128


def write_codes(places, y, delta, factor, out):
    start = pl.program_id(0) * BLOCK
    d, f = delta[...], factor[...]

    @pl.loop(0, BLOCK // 8)
    def _(i):
        for u in range(8):
            out[i * 8 + u] = (y[places[start + i * 8 + u]] - d) * f


def on_device(raw, slot_angle, segment_of, seg_owner, flat, dark, row_order, bin_counts):
    smem = pl.BlockSpec(memory_space=pltpu.SMEM)
    vmem = pl.BlockSpec(memory_space=pltpu.VMEM)
    hbm = pl.BlockSpec(memory_space=pl.ANY)
    tile = jax.ShapeDtypeStruct((8, 128), jnp.float32)
    dma = pltpu.SemaphoreType.DMA
    y, delta, factor, places = pl.pallas_call(
        exchange,
        name="exchange",
        out_shape=(
            jax.ShapeDtypeStruct((ANGLES, 8, 128), jnp.float32),
            tile,
            tile,
            jax.ShapeDtypeStruct((8, 128), jnp.int32),
        ),
        in_specs=[smem] * 5 + [hbm] * 3,
        out_specs=(vmem,) * 4,
        scratch_shapes=[
            pltpu.VMEM((HALF, ROWS, COLS_DEV), jnp.bfloat16),
            pltpu.VMEM((HALF, ROWS, COLS_DEV), jnp.bfloat16),
            pltpu.VMEM((PARTS, PROJ, PAIRS, 16, 128), jnp.bfloat16),
            pltpu.VMEM((PARTS, PROJ, PAIRS, 16, 128), jnp.bfloat16),
            pltpu.VMEM((SEGS, ROWS, COLS_DEV), jnp.float32),
            pltpu.VMEM((SEGS, ROWS, COLS_DEV), jnp.float32),
            pltpu.VMEM((256, 256), jnp.float32),
            pltpu.VMEM((256, 256), jnp.bfloat16),
            pltpu.VMEM((PROJ, SEGS, 16, 128), jnp.int16),
            pltpu.VMEM((CHIPS, SEGS, 16, 128), jnp.int16),
            pltpu.VMEM((CHIPS, SEGS, 16, 128), jnp.int16),
            pltpu.VMEM((CHIPS, SEGS, 16, 128), jnp.int16),
            pltpu.VMEM((SEGS, 8, 128), jnp.float32),
            pltpu.VMEM((SEGS, 8, 128), jnp.float32),
            pltpu.VMEM((DET, 8, 128), jnp.float32),
            pltpu.VMEM((DET, 8, 128), jnp.float32),
            dma((PARTS,)),
            dma((2,)),
            dma((PARTS,)),
            dma((PARTS,)),
            dma((PARTS, PROJ)),
            dma((PARTS, PROJ)),
            dma((2,)),
            dma((CHIPS,)),
            dma((CHIPS,)),
            dma((2, DET)),
            dma((2, DET)),
        ],
        compiler_params=pltpu.CompilerParams(
            collective_id=0, has_side_effects=True, vmem_limit_bytes=40 << 20
        ),
    )(slot_angle, segment_of, seg_owner, row_order, bin_counts, raw, flat, dark)
    whole = pl.BlockSpec((ANGLES, 8, 128), lambda i, places: (0, 0, 0))
    small = pl.BlockSpec((8, 128), lambda i, places: (0, 0))
    codes = pl.pallas_call(
        write_codes,
        name="write_codes",
        out_shape=jax.ShapeDtypeStruct((ANGLES, 8, 128), jnp.float32),
        grid_spec=pltpu.PrefetchScalarGridSpec(
            num_scalar_prefetch=1,
            grid=(ANGLES // BLOCK,),
            in_specs=[whole, small, small],
            out_specs=pl.BlockSpec((BLOCK, 8, 128), lambda i, places: (i, 0, 0)),
        ),
        compiler_params=pltpu.CompilerParams(vmem_limit_bytes=32 << 20),
    )(places.reshape(ANGLES), y, delta, factor)
    return codes.reshape(ANGLES, TILES, 2, 128).transpose(0, 2, 1, 3).reshape(ANGLES, 2, COLS_DEV)


def solution(mesh):
    return jax.shard_map(
        on_device,
        mesh=mesh,
        in_specs=(
            P("proj", None, "det"),
            P(),
            P(),
            P(),
            P("proj", None, "det"),
            P("proj", None, "det"),
            P(),
            P(),
        ),
        out_specs=P(None, "proj", "det"),
        check_vma=False,
    )
```

```python
import jax
import jax.numpy as jnp
from jax import lax
from jax.experimental import pallas as pl
from jax.experimental.pallas import tpu as pltpu
from jax.sharding import PartitionSpec as P

MESH = pl.DeviceIdType.MESH

SLOTS = 64
ANGLES = 1024
ROWS = 64
COLS_DEV = 512
COLS = 2048
SEGS = 8
RIM = 8
PROJ = 32
CHIPS = 16
DET = 4
TILES = COLS_DEV // 128
PARTS = 8
FRAMES = SLOTS // PARTS
PAIRS = FRAMES // 2
EARLY = 4
EPSILON = 1e-6
DARK_STEP = 0.2 / 65535.0
FLAT_STEP = 1.0 / 65535.0
STEPS = (
    (2, 2), (1, 2), (2, 1), (3, 2), (2, 3), (1, 1), (3, 3), (1, 3),
    (3, 1), (0, 2), (2, 0), (0, 1), (1, 0), (0, 3), (3, 0),
)


def stack_tiles(frame):
    return jnp.concatenate([frame[:, 128 * t : 128 * (t + 1)] for t in range(TILES)], axis=0)


def coded(field, low, step):
    q = jnp.floor((field - low) * (1.0 / step) + 0.5)
    q = jnp.clip(q, 0.0, 65535.0)
    high = jnp.floor(q * (1.0 / 256.0))
    return high.astype(jnp.bfloat16), (q - 256.0 * high).astype(jnp.bfloat16)


def exchange(
    slot_angle_h,
    segment_of_h,
    seg_owner_h,
    row_order_h,
    bin_counts_h,
    raw,
    flat,
    dark,
    corrected_out,
    factor_out,
    slot_angle,
    segment_of,
    seg_owner,
    row_order,
    bin_counts,
    segs,
    places,
    places_v,
    frames,
    own,
    away,
    mate_in,
    recv,
    y_v,
    flat_v,
    dark_v,
    pick_f,
    pick,
    fsend,
    fpart,
    frecv,
    dark_s,
    logflat_s,
    profs,
    sums,
    int_sem,
    load_sem,
    field_sem,
    place_sem,
    swap_ssem,
    swap_rsem,
    send_sem,
    recv_sem,
    fswap_sem,
    fsend_sem,
    frecv_sem,
    small_ssem,
    small_rsem,
):
    proj = lax.axis_index("proj")
    det = lax.axis_index("det")
    core = proj % 2
    chip = proj // 2
    col = chip % 4
    lay = chip // 4
    mate = proj + 1 - 2 * core

    def chip_at(step):
        return (lay + step[0]) % 4 * 4 + (col + step[1]) % 4

    def chip_back(t):
        return (lay + 4 - t // 4) % 4 * 4 + (col + 4 - t % 4) % 4

    ints = []
    for i, (source, target) in enumerate(
        (
            (row_order_h, row_order),
            (slot_angle_h, slot_angle),
            (seg_owner_h, seg_owner),
            (segment_of_h, segment_of),
            (bin_counts_h, bin_counts),
        )
    ):
        ints.append(pltpu.make_async_copy(source, target, int_sem.at[i]))
        ints[-1].start()
    order = [q for i in range(PARTS // 2) for q in (PARTS - 1 - i, i)]
    loads = {}
    for q in order:
        block = pl.ds(FRAMES * q, FRAMES)
        loads[q] = pltpu.make_async_copy(raw.at[block], frames.at[block], load_sem.at[q])
        loads[q].start()
    flat_copy = pltpu.make_async_copy(flat, flat_v, field_sem.at[0])
    dark_copy = pltpu.make_async_copy(dark, dark_v, field_sem.at[1])
    flat_copy.start()
    dark_copy.start()

    barrier = pltpu.get_barrier_semaphore()
    for step in STEPS:
        pl.semaphore_signal(
            barrier, inc=1, device_id=(2 * chip_at(step) + core, det), device_id_type=MESH
        )
    for t in range(1, DET):
        pl.semaphore_signal(
            barrier, inc=1, device_id=(proj, (det + t) % DET), device_id_type=MESH
        )
    pl.semaphore_signal(barrier, inc=1, device_id=(mate, det), device_id_type=MESH)

    for copy in ints:
        copy.wait()

    sub = lax.broadcasted_iota(jnp.int32, (8, 256), 0)
    lane = lax.broadcasted_iota(jnp.int32, (8, 256), 1)

    @pl.loop(0, PROJ)
    def _(i):
        p = 2 * (i % CHIPS) + (core + i // CHIPS) % 2
        row = jnp.where(sub % 2 == 0, row_order[2 * p], row_order[2 * p + 1])
        hit = lane == row + (sub // 2) * ROWS
        pick_f[pl.ds(pl.multiple_of(8 * i, 8), 8), :] = jnp.where(hit, 1.0, 0.0)

    pick[...] = pick_f[...].astype(jnp.bfloat16)

    def permute(q):
        loads[q].wait()

        @pl.loop(0, PAIRS)
        def _(j):
            first = stack_tiles(frames[FRAMES * q + 2 * j])
            second = stack_tiles(frames[FRAMES * q + 2 * j + 1])
            moved = jnp.dot(
                pick[...], jnp.concatenate([first, second], axis=1), preferred_element_type=jnp.float32
            ).reshape(PROJ, 8, 256)
            here, there = moved[:CHIPS], moved[CHIPS:]
            own[q, :, j] = jnp.concatenate([here[:, :, :128], here[:, :, 128:]], axis=1).astype(
                jnp.bfloat16
            )
            away[PARTS - 1 - q, :, PAIRS - 1 - j] = jnp.concatenate(
                [there[:, :, 128:], there[:, :, :128]], axis=1
            ).astype(jnp.bfloat16)

    def swap(part):
        return pltpu.make_async_remote_copy(
            src_ref=away.at[part],
            dst_ref=mate_in.at[part],
            send_sem=swap_ssem.at[part],
            recv_sem=swap_rsem.at[part],
            device_id=(mate, det),
            device_id_type=MESH,
        )

    sub16 = lax.broadcasted_iota(jnp.int32, (16, 128), 0)

    def merge(part):
        swap(part).wait_recv()

        @pl.loop(0, PAIRS)
        def _(j):
            k = SLOTS * proj + FRAMES * part + 2 * j
            keep = jnp.where(
                sub16 < 8,
                jnp.where(slot_angle[k] < ANGLES, 1.0, 0.0),
                jnp.where(slot_angle[k + 1] < ANGLES, 1.0, 0.0),
            )
            mine = keep.astype(jnp.bfloat16)
            other = (1.0 - keep).astype(jnp.bfloat16)
            own[part, :, j] = own[part, :, j] * mine + mate_in[part, :, j] * other

    def frame_copy(part, t, target):
        return pltpu.make_async_remote_copy(
            src_ref=own.at[part, target],
            dst_ref=recv.at[part, chip],
            send_sem=send_sem.at[part, t],
            recv_sem=recv_sem.at[part, chip],
            device_id=(2 * target + core, det),
            device_id_type=MESH,
        )

    def ship(part):
        merge(part)
        for t, step in enumerate(STEPS):
            frame_copy(part, t, chip_at(step)).start()

    def join_copy():
        return pltpu.make_async_remote_copy(
            src_ref=fsend.at[pl.ds(CHIPS, CHIPS)],
            dst_ref=fpart,
            send_sem=fswap_sem.at[0],
            recv_sem=fswap_sem.at[1],
            device_id=(mate, det),
            device_id_type=MESH,
        )

    def field_copy(t, target):
        return pltpu.make_async_remote_copy(
            src_ref=fsend.at[target],
            dst_ref=frecv.at[chip],
            send_sem=fsend_sem.at[t],
            recv_sem=frecv_sem.at[chip],
            device_id=(2 * target + core, det),
            device_id_type=MESH,
        )

    def code_fields():
        flat_copy.wait()
        dark_copy.wait()

        @pl.loop(0, SEGS)
        def _(s):
            mine = jnp.where(seg_owner[s] == proj, 1.0, 0.0)
            moved = []
            for ref, low, step in ((flat_v, 1.0, FLAT_STEP), (dark_v, 0.0, DARK_STEP)):
                high, small = coded(stack_tiles(ref[s]), low, step)
                both = jnp.dot(
                    pick[...], jnp.concatenate([high, small], axis=1), preferred_element_type=jnp.float32
                )
                code = (both[:, :128] * 256.0 + both[:, 128:] - 32768.0) * mine
                moved.append(code.reshape(PROJ, 8, 128))
            pair = jnp.concatenate(moved, axis=1)
            fsend[:, s] = pair.astype(jnp.int32).astype(jnp.int16)

        join_copy().start()

    def ship_fields():
        join_copy().wait()

        @pl.loop(0, CHIPS)
        def _(i):
            fsend[i] = (fsend[i].astype(jnp.int32) + fpart[i].astype(jnp.int32)).astype(jnp.int16)

        for t, step in enumerate(STEPS):
            field_copy(t, chip_at(step)).start()
        frecv[chip] = fsend[chip]

    def take_fields():
        @pl.loop(1, CHIPS)
        def _(t):
            source = chip_back(t)
            pltpu.make_async_remote_copy(
                src_ref=fsend.at[source],
                dst_ref=frecv.at[source],
                send_sem=fsend_sem.at[t - 1],
                recv_sem=frecv_sem.at[source],
                device_id=(2 * source + core, det),
                device_id_type=MESH,
            ).wait()

        @pl.loop(0, SEGS)
        def _(s):
            total = frecv[0, s].astype(jnp.int32)
            for i in range(1, CHIPS):
                total = total + frecv[i, s].astype(jnp.int32)
            code = (total + 32768).astype(jnp.float32)
            f = 1.0 + code[:8] * FLAT_STEP
            d = code[8:] * DARK_STEP
            dark_s[s] = d
            logflat_s[s] = jnp.log(f - d)

    for q in order[:EARLY]:
        permute(q)
    pl.semaphore_wait(barrier, len(STEPS) + DET)
    for q in order[:EARLY]:
        swap(PARTS - 1 - q).start()

    def more(q):
        permute(q)
        swap(PARTS - 1 - q).start()

    ship(0)
    more(order[4])
    ship(1)
    more(order[5])
    code_fields()
    ship(2)
    more(order[6])
    ship_fields()
    more(order[7])
    for part in range(3, PARTS):
        ship(part)

    sub = lax.broadcasted_iota(jnp.int32, (8, 128), 0)
    lane = lax.broadcasted_iota(jnp.int32, (8, 128), 1)
    angle_id = sub * 128 + lane

    def locate(i, found):
        source = 2 * (i // (SLOTS // 4)) + core
        pair = source + 1 - 2 * core
        found = list(found)
        for u in range(4):
            k = i % (SLOTS // 4) * 4 + u
            here = slot_angle[SLOTS * source + k]
            there = slot_angle[SLOTS * pair + SLOTS - 1 - k]
            angle = jnp.where(here < ANGLES, here, there)
            segs[i * 4 + u] = segment_of[angle]
            found[u] = jnp.where(angle_id == angle, i * 4 + u, found[u])
        return tuple(found)

    found = lax.fori_loop(0, ANGLES // 4, locate, (jnp.zeros((8, 128), jnp.int32),) * 4)
    places_v[...] = jnp.maximum(jnp.maximum(found[0], found[1]), jnp.maximum(found[2], found[3]))
    place_copy = pltpu.make_async_copy(places_v, places, place_sem.at[0])
    place_copy.start()

    take_fields()

    def absorb(ref, part, source, accs):
        accs = list(accs)
        for j in range(PAIRS):
            x = ref[part, source, j].astype(jnp.float32)
            for f in range(2):
                slot = source * SLOTS + FRAMES * part + 2 * j + f
                s = segs[slot]
                y = logflat_s[s] - jnp.log(x[8 * f : 8 * f + 8] - dark_s[s])
                y = y.astype(jnp.bfloat16).astype(jnp.float32)
                y_v[slot] = y
                accs[f] = accs[f] + y
        return tuple(accs)

    zero = jnp.zeros((8, 128), jnp.float32)
    accs = (zero, zero)
    for part in range(PARTS):
        accs = absorb(own, part, chip, accs)

        def step(t, accs, part=part):
            source = chip_back(t)
            pltpu.make_async_remote_copy(
                src_ref=own.at[part, source],
                dst_ref=recv.at[part, source],
                send_sem=send_sem.at[part, t - 1],
                recv_sem=recv_sem.at[part, source],
                device_id=(2 * source + core, det),
                device_id_type=MESH,
            ).wait()
            return absorb(recv, part, source, accs)

        accs = lax.fori_loop(1, CHIPS, step, accs)
        swap(part).wait_send()
    place_copy.wait()
    profile = (accs[0] + accs[1]) * (1.0 / ANGLES)

    def share(ref, which, t):
        return pltpu.make_async_remote_copy(
            src_ref=ref.at[det],
            dst_ref=ref.at[det],
            send_sem=small_ssem.at[which, t],
            recv_sem=small_rsem.at[which, det],
            device_id=(proj, (det + t) % DET),
            device_id_type=MESH,
        )

    def shared(ref, which, t):
        source = (det + t) % DET
        return pltpu.make_async_remote_copy(
            src_ref=ref.at[source],
            dst_ref=ref.at[source],
            send_sem=small_ssem.at[which, t],
            recv_sem=small_rsem.at[which, source],
            device_id=(proj, source),
            device_id_type=MESH,
        )

    profs[det] = profile
    for t in (1, 3, 2):
        share(profs, 0, t).start()
    shared(profs, 0, 1).wait_recv()
    shared(profs, 0, 3).wait_recv()
    shared(profs, 0, 2).wait_recv()
    before = profs[(det + DET - 1) % DET]
    after = profs[(det + 1) % DET]
    before = jnp.where(det > 0, before, jnp.zeros_like(before))
    after = jnp.where(det < DET - 1, after, jnp.zeros_like(after))
    low = jnp.where(sub < 2, pltpu.roll(before, 2, 0), pltpu.roll(profile, 2, 0))
    high = jnp.where(sub >= 6, pltpu.roll(after, 6, 0), pltpu.roll(profile, 6, 0))
    window = profile
    for o in range(1, RIM + 1):
        window = window + jnp.where(lane >= o, pltpu.roll(profile, o, 1), pltpu.roll(low, o, 1))
        window = window + jnp.where(
            lane < 128 - o, pltpu.roll(profile, 128 - o, 1), pltpu.roll(high, 128 - o, 1)
        )
    column = det * COLS_DEV + (sub // 2) * 128 + lane
    counted = jnp.minimum(column + RIM, COLS - 1) - jnp.maximum(column - RIM, 0) + 1
    delta = profile - window / counted.astype(jnp.float32)

    def magnitude(i, accs):
        return tuple(
            accs[u] + jnp.abs(y_v[i * 16 + u] - delta) + jnp.abs(y_v[i * 16 + 8 + u] - delta)
            for u in range(8)
        )

    accs = lax.fori_loop(0, ANGLES // 16, magnitude, (zero,) * 8)
    total = ((accs[0] + accs[1]) + (accs[2] + accs[3])) + ((accs[4] + accs[5]) + (accs[6] + accs[7]))
    sums[det] = total
    for t in (2, 1, 3):
        share(sums, 1, t).start()

    @pl.loop(0, ANGLES // 16)
    def _(i):
        for u in range(16):
            a = 16 * (i % 8) + u
            corrected_out[i * 16 + u] = y_v[places[i // 8, a]] - delta

    for t in range(1, DET):
        shared(sums, 1, t).wait_recv()
    total = (sums[0] + sums[1]) + (sums[2] + sums[3])
    rows = jnp.broadcast_to(jnp.sum(total, axis=1, keepdims=True), (8, 128))
    rows = rows + pltpu.roll(rows, 4, 0)
    rows = rows + pltpu.roll(rows, 2, 0)
    scale = rows * (1.0 / (ANGLES * COLS)) + EPSILON
    bins = jnp.where(
        sub % 2 == 0,
        bin_counts[row_order[2 * proj]],
        bin_counts[row_order[2 * proj + 1]],
    ).astype(jnp.float32)
    factor_out[...] = bins / scale

    for which, ref in enumerate((profs, sums)):
        for t in range(1, DET):
            share(ref, which, t).wait_send()


BLOCK = 128
DEPTH = 4


def write_codes(corrected, factor, out, block, sem):
    f = factor[...]

    def copy(i):
        return pltpu.make_async_copy(
            block.at[i % DEPTH], out.at[pl.ds(i * BLOCK, BLOCK)], sem.at[i % DEPTH]
        )

    @pl.loop(0, ANGLES // BLOCK)
    def _(i):
        @pl.when(i >= DEPTH)
        def _():
            copy(i - DEPTH).wait()

        @pl.loop(0, BLOCK // 16)
        def _(k):
            for u in range(16):
                block[i % DEPTH, k * 16 + u] = corrected[i * BLOCK + k * 16 + u] * f

        copy(i).start()

    @pl.loop(ANGLES // BLOCK - DEPTH, ANGLES // BLOCK)
    def _(i):
        copy(i).wait()


def on_device(raw, slot_angle, segment_of, seg_owner, flat, dark, row_order, bin_counts):
    vmem = pl.BlockSpec(memory_space=pltpu.VMEM)
    hbm = pl.BlockSpec(memory_space=pltpu.HBM)
    dma = pltpu.SemaphoreType.DMA
    corrected, factor = pl.pallas_call(
        exchange,
        name="exchange",
        out_shape=(
            jax.ShapeDtypeStruct((ANGLES, 8, 128), jnp.float32),
            jax.ShapeDtypeStruct((8, 128), jnp.float32),
        ),
        in_specs=[hbm] * 8,
        out_specs=(vmem,) * 2,
        scratch_shapes=[
            pltpu.SMEM((PROJ * SLOTS,), jnp.int32),
            pltpu.SMEM((ANGLES,), jnp.int32),
            pltpu.SMEM((SEGS,), jnp.int32),
            pltpu.SMEM((ROWS,), jnp.int32),
            pltpu.SMEM((ROWS,), jnp.int32),
            pltpu.SMEM((ANGLES,), jnp.int32),
            pltpu.SMEM((8, 128), jnp.int32),
            pltpu.VMEM((8, 128), jnp.int32),
            pltpu.VMEM((SLOTS, ROWS, COLS_DEV), jnp.bfloat16),
            pltpu.VMEM((PARTS, CHIPS, PAIRS, 16, 128), jnp.bfloat16),
            pltpu.VMEM((PARTS, CHIPS, PAIRS, 16, 128), jnp.bfloat16),
            pltpu.VMEM((PARTS, CHIPS, PAIRS, 16, 128), jnp.bfloat16),
            pltpu.VMEM((PARTS, CHIPS, PAIRS, 16, 128), jnp.bfloat16),
            pltpu.VMEM((ANGLES, 8, 128), jnp.float32),
            pltpu.VMEM((SEGS, ROWS, COLS_DEV), jnp.float32),
            pltpu.VMEM((SEGS, ROWS, COLS_DEV), jnp.float32),
            pltpu.VMEM((256, 256), jnp.float32),
            pltpu.VMEM((256, 256), jnp.bfloat16),
            pltpu.VMEM((PROJ, SEGS, 16, 128), jnp.int16),
            pltpu.VMEM((CHIPS, SEGS, 16, 128), jnp.int16),
            pltpu.VMEM((CHIPS, SEGS, 16, 128), jnp.int16),
            pltpu.VMEM((SEGS, 8, 128), jnp.float32),
            pltpu.VMEM((SEGS, 8, 128), jnp.float32),
            pltpu.VMEM((DET, 8, 128), jnp.float32),
            pltpu.VMEM((DET, 8, 128), jnp.float32),
            dma((5,)),
            dma((PARTS,)),
            dma((2,)),
            dma((1,)),
            dma((PARTS,)),
            dma((PARTS,)),
            dma((PARTS, CHIPS)),
            dma((PARTS, CHIPS)),
            dma((2,)),
            dma((CHIPS,)),
            dma((CHIPS,)),
            dma((2, DET)),
            dma((2, DET)),
        ],
        compiler_params=pltpu.CompilerParams(
            collective_id=0, has_side_effects=True, vmem_limit_bytes=40 << 20
        ),
    )(
        *(
            pltpu.with_memory_space_constraint(a, pltpu.HBM)
            for a in (slot_angle, segment_of, seg_owner, row_order, bin_counts, raw, flat, dark)
        )
    )
    codes = pl.pallas_call(
        write_codes,
        name="write_codes",
        out_shape=jax.ShapeDtypeStruct((ANGLES, 8, 128), jnp.float32),
        in_specs=[vmem, vmem],
        out_specs=hbm,
        scratch_shapes=[pltpu.VMEM((DEPTH, BLOCK, 8, 128), jnp.float32), dma((DEPTH,))],
        compiler_params=pltpu.CompilerParams(vmem_limit_bytes=16 << 20),
    )(corrected, factor)
    return codes.reshape(ANGLES, TILES, 2, 128).transpose(0, 2, 1, 3).reshape(ANGLES, 2, COLS_DEV)


def solution(mesh):
    return jax.shard_map(
        on_device,
        mesh=mesh,
        in_specs=(
            P("proj", None, "det"),
            P(),
            P(),
            P(),
            P("proj", None, "det"),
            P("proj", None, "det"),
            P(),
            P(),
        ),
        out_specs=P(None, "proj", "det"),
        check_vma=False,
    )
```

```python
import jax
import jax.numpy as jnp
from jax import lax
from jax.experimental import pallas as pl
from jax.experimental.pallas import tpu as pltpu
from jax.sharding import PartitionSpec as P

MESH = pl.DeviceIdType.MESH

SLOTS = 64
ANGLES = 1024
ROWS = 64
COLS_DEV = 512
COLS = 2048
SEGS = 8
RIM = 8
PROJ = 32
CHIPS = 16
DET = 4
TILES = COLS_DEV // 128
PARTS = 8
FRAMES = SLOTS // PARTS
PAIRS = FRAMES // 2
HEAD = 1
BATCH = 4
ARRANGED = 20
HALVES = 2
RING = 4
HSEGS = SEGS // HALVES
EPSILON = 1e-6
DARK_STEP = 0.2 / 65535.0
FLAT_STEP = 1.0 / 65535.0
STEPS = (
    (2, 2), (1, 2), (2, 1), (3, 2), (2, 3), (1, 1), (3, 3), (1, 3),
    (3, 1), (0, 2), (2, 0), (0, 1), (1, 0), (0, 3), (3, 0),
)


def stack_tiles(frame):
    return jnp.concatenate([frame[:, 128 * t : 128 * (t + 1)] for t in range(TILES)], axis=0)


def coded(field, low, step):
    q = jnp.floor((field - low) * (1.0 / step) + 0.5)
    q = jnp.clip(q, 0.0, 65535.0)
    high = jnp.floor(q * (1.0 / 256.0))
    return high.astype(jnp.bfloat16), (q - 256.0 * high).astype(jnp.bfloat16)


def exchange(
    slot_angle_h,
    segment_of_h,
    seg_owner_h,
    row_order_h,
    bin_counts_h,
    raw,
    flat,
    dark,
    ordered_out,
    delta_out,
    factor_out,
    slot_angle,
    seg_owner,
    row_order,
    bin_counts,
    angle_v,
    segment_v,
    segs,
    segs_v,
    places,
    places_v,
    frames,
    own,
    away,
    mate_in,
    recv,
    y_v,
    flat_v,
    dark_v,
    pick_f,
    pick,
    fsend,
    fmate,
    fpart,
    fring,
    fnext,
    flast,
    edges,
    dark_s,
    logflat_s,
    profs,
    sums,
    int_sem,
    load_sem,
    field_sem,
    place_sem,
    swap_ssem,
    swap_rsem,
    send_sem,
    recv_sem,
    fswap_sem,
    fring_sem,
    flast_sem,
    small_sem,
):
    proj = lax.axis_index("proj")
    det = lax.axis_index("det")
    core = proj % 2
    chip = proj // 2
    col = chip % 4
    lay = chip // 4
    mate = proj + 1 - 2 * core

    def chip_at(step):
        return (lay + step[0]) % 4 * 4 + (col + step[1]) % 4

    barrier = pltpu.get_barrier_semaphore()
    for step in STEPS:
        pl.semaphore_signal(
            barrier, inc=1, device_id=(2 * chip_at(step) + core, det), device_id_type=MESH
        )
    for t in range(1, DET):
        pl.semaphore_signal(
            barrier, inc=1, device_id=(proj, (det + t) % DET), device_id_type=MESH
        )
    pl.semaphore_signal(barrier, inc=1, device_id=(mate, det), device_id_type=MESH)

    ints = []
    for i, (source, target) in enumerate(
        (
            (row_order_h, row_order),
            (slot_angle_h, slot_angle),
            (seg_owner_h, seg_owner),
            (bin_counts_h, bin_counts),
            (slot_angle_h, angle_v),
            (segment_of_h, segment_v),
        )
    ):
        ints.append(pltpu.make_async_copy(source, target, int_sem.at[i]))
        ints[-1].start()
    order = [q for i in range(PARTS // 2) for q in (PARTS - 1 - i, i)]
    loads = {}
    for q in order:
        block = pl.ds(FRAMES * q, FRAMES)
        loads[q] = pltpu.make_async_copy(raw.at[block], frames.at[block], load_sem.at[q])
        loads[q].start()
    flat_copy = pltpu.make_async_copy(flat, flat_v, field_sem.at[0])
    dark_copy = pltpu.make_async_copy(dark, dark_v, field_sem.at[1])
    flat_copy.start()
    dark_copy.start()

    for copy in ints:
        copy.wait()

    sub = lax.broadcasted_iota(jnp.int32, (8, 256), 0)
    lane = lax.broadcasted_iota(jnp.int32, (8, 256), 1)

    @pl.loop(0, PROJ)
    def _(i):
        p = 2 * (i % CHIPS) + (core + i // CHIPS) % 2
        row = jnp.where(sub % 2 == 0, row_order[2 * p], row_order[2 * p + 1])
        hit = lane == row + (sub // 2) * ROWS
        pick_f[pl.ds(pl.multiple_of(8 * i, 8), 8), :] = jnp.where(hit, 1.0, 0.0)

    pick[...] = pick_f[...].astype(jnp.bfloat16)

    def permute(q):
        loads[q].wait()

        @pl.loop(0, PAIRS // 2)
        def _(i):
            block = [stack_tiles(frames[FRAMES * q + 4 * i + f]) for f in range(4)]
            moved = jnp.dot(
                pick[...], jnp.concatenate(block, axis=1), preferred_element_type=jnp.float32
            ).reshape(PROJ, 8, 512)
            part = [moved[:, :, 128 * f : 128 * (f + 1)] for f in range(4)]
            for j in range(2):
                first, second = part[2 * j], part[2 * j + 1]
                own[q, :, 2 * i + j] = jnp.concatenate(
                    [first[:CHIPS], second[:CHIPS]], axis=1
                ).astype(jnp.bfloat16)
                away[PARTS - 1 - q, :, PAIRS - 1 - 2 * i - j] = jnp.concatenate(
                    [second[CHIPS:], first[CHIPS:]], axis=1
                ).astype(jnp.bfloat16)

    def swap(part, first=0, count=PAIRS, which=None):
        which = part if which is None else which
        pairs = pl.ds(first, count)
        return pltpu.make_async_remote_copy(
            src_ref=away.at[part, :, pairs],
            dst_ref=mate_in.at[part, :, pairs],
            send_sem=swap_ssem.at[which],
            recv_sem=swap_rsem.at[which],
            device_id=(mate, det),
            device_id_type=MESH,
        )

    pieces = ((0, HEAD, PARTS), (HEAD, PAIRS - HEAD, 0))

    sub16 = lax.broadcasted_iota(jnp.int32, (16, 128), 0)

    def merge(part, first=0, count=PAIRS):
        @pl.loop(first, first + count)
        def _(j):
            k = SLOTS * core + FRAMES * part + 2 * j
            keep = jnp.where(
                sub16 < 8,
                jnp.where(slot_angle[chip, k] < ANGLES, 1.0, 0.0),
                jnp.where(slot_angle[chip, k + 1] < ANGLES, 1.0, 0.0),
            )
            mine = keep.astype(jnp.bfloat16)
            other = (1.0 - keep).astype(jnp.bfloat16)
            merged = own[part, :, j] * mine + mate_in[part, :, j] * other
            own[part, :, j] = merged

    def frame_copy(part, target, first=0, count=PAIRS):
        pairs = pl.ds(first, count)
        return pltpu.make_async_remote_copy(
            src_ref=own.at[part, target, pairs],
            dst_ref=recv.at[part, chip, pairs],
            send_sem=send_sem.at[part],
            recv_sem=recv_sem.at[part],
            device_id=(2 * target + core, det),
            device_id_type=MESH,
        )

    def ship(part, first=0, count=PAIRS, which=None):
        swap(part, first, count, which).wait_recv()
        merge(part, first, count)
        for step in STEPS:
            frame_copy(part, chip_at(step), first, count).start()

    def all_frames(part):
        chips = pl.ds(0, CHIPS - 1)
        return pltpu.make_async_remote_copy(
            src_ref=own.at[part, chips],
            dst_ref=recv.at[part, chips],
            send_sem=send_sem.at[part],
            recv_sem=recv_sem.at[part],
            device_id=(mate, det),
            device_id_type=MESH,
        )

    def join_copy():
        return pltpu.make_async_remote_copy(
            src_ref=fmate,
            dst_ref=fpart,
            send_sem=fswap_sem.at[0],
            recv_sem=fswap_sem.at[1],
            device_id=(mate, det),
            device_id_type=MESH,
        )

    places_of = ((col, lay), (lay, col))

    def ring_copy(half, d):
        mine = places_of[half][0]
        there = (mine + d) % RING
        target = lay * 4 + there if half == 0 else there * 4 + col
        return pltpu.make_async_remote_copy(
            src_ref=fsend.at[half, there],
            dst_ref=fring.at[half, mine],
            send_sem=fring_sem.at[half, 0],
            recv_sem=fring_sem.at[half, 1],
            device_id=(2 * target + core, det),
            device_id_type=MESH,
        )

    def last_copy(half, d):
        mine = places_of[half][1]
        there = (mine + d) % RING
        target = there * 4 + col if half == 0 else lay * 4 + there
        return pltpu.make_async_remote_copy(
            src_ref=fnext.at[half, there],
            dst_ref=flast.at[half, mine],
            send_sem=flast_sem.at[half, 0],
            recv_sem=flast_sem.at[half, 1],
            device_id=(2 * target + core, det),
            device_id_type=MESH,
        )

    def all_ring(half):
        others = pl.ds(0, RING - 1)
        return pltpu.make_async_remote_copy(
            src_ref=fsend.at[half, others],
            dst_ref=fring.at[half, others],
            send_sem=fring_sem.at[half, 0],
            recv_sem=fring_sem.at[half, 1],
            device_id=(mate, det),
            device_id_type=MESH,
        )

    def all_last(half):
        others = pl.ds(0, RING - 1)
        return pltpu.make_async_remote_copy(
            src_ref=fnext.at[half, others],
            dst_ref=flast.at[half, others],
            send_sem=flast_sem.at[half, 0],
            recv_sem=flast_sem.at[half, 1],
            device_id=(mate, det),
            device_id_type=MESH,
        )

    def code_fields():
        flat_copy.wait()
        dark_copy.wait()
        for half in range(HALVES):

            @pl.loop(0, HSEGS)
            def _(h, half=half):
                s = half * HSEGS + h
                mine = jnp.where(seg_owner[s] == proj, 1.0, 0.0)
                moved = []
                for ref, low, step in ((flat_v, 1.0, FLAT_STEP), (dark_v, 0.0, DARK_STEP)):
                    high, small = coded(stack_tiles(ref[s]), low, step)
                    both = jnp.dot(
                        pick[...],
                        jnp.concatenate([high, small], axis=1),
                        preferred_element_type=jnp.float32,
                    )
                    code = (both[:, :128] * 256.0 + both[:, 128:] - 32768.0) * mine
                    moved.append(code.reshape(PROJ, 8, 128))
                pair = jnp.concatenate(moved, axis=1).astype(jnp.int32).astype(jnp.int16)
                for z in range(RING):
                    for x in range(RING):
                        outer, inner = (x, z) if half == 0 else (z, x)
                        fsend[half, outer, inner, h] = pair[z * RING + x]
                        fmate[half, outer, inner, h] = pair[CHIPS + z * RING + x]

    def ship_fields():
        join_copy().wait()
        for half in range(HALVES):
            mine = places_of[half][0]

            @pl.loop(0, RING)
            def _(o, half=half):
                fsend[half, o] = (
                    fsend[half, o].astype(jnp.int32) + fpart[half, o].astype(jnp.int32)
                ).astype(jnp.int16)

            fring[half, mine] = fsend[half, mine]
        for d in (2, 1, 3):
            for half in range(HALVES):
                ring_copy(half, d).start()

    def pass_fields():
        for half in range(HALVES):
            all_ring(half).wait_recv()
            mine = places_of[half][1]

            @pl.loop(0, RING)
            def _(i, half=half):
                total = fring[half, 0, i].astype(jnp.int32)
                for o in range(1, RING):
                    total = total + fring[half, o, i].astype(jnp.int32)
                fnext[half, i] = total.astype(jnp.int16)

            flast[half, mine] = fnext[half, mine]
            for d in (2, 1, 3):
                last_copy(half, d).start()

    def take_fields():
        for half in range(HALVES):
            all_last(half).wait_recv()
            total = flast[half, 0].astype(jnp.int32)
            for i in range(1, RING):
                total = total + flast[half, i].astype(jnp.int32)
            code = (total + 32768).astype(jnp.float32)
            f = 1.0 + code[:, :8] * FLAT_STEP
            d = code[:, 8:] * DARK_STEP
            dark_s[half * HSEGS : (half + 1) * HSEGS] = d
            logflat_s[half * HSEGS : (half + 1) * HSEGS] = jnp.log(f - d)
            all_ring(half).wait_send()
            all_last(half).wait_send()

    def more(q):
        permute(q)
        swap(PARTS - 1 - q).start()

    for q in order[:2]:
        permute(q)
    pl.semaphore_wait(barrier, len(STEPS) + DET)
    for first, count, which in pieces:
        swap(0, first, count, which).start()
    swap(PARTS - 1).start()
    for first, count, which in pieces:
        ship(0, first, count, which)
    more(order[2])
    more(order[3])
    code_fields()
    join_copy().start()
    ship(1)
    ship_fields()
    more(order[4])
    more(order[5])
    ship(2)
    more(order[6])
    more(order[7])
    ship(3)
    pass_fields()
    for part in range(4, PARTS):
        ship(part)

    sub = lax.broadcasted_iota(jnp.int32, (8, 128), 0)
    lane = lax.broadcasted_iota(jnp.int32, (8, 128), 1)
    zero = jnp.zeros((8, 128), jnp.float32)

    def locate():
        lane16 = lax.broadcasted_iota(jnp.int32, (CHIPS, 128), 1)
        angle = angle_v[...]
        mirrored = angle
        for bit in (1, 2, 4, 8, 16, 32, 64):
            mirrored = jnp.where(
                lane16 & bit == 0, pltpu.roll(mirrored, 128 - bit, 1), pltpu.roll(mirrored, bit, 1)
            )
        angle = jnp.where(angle < ANGLES, angle, mirrored)
        angle = jnp.where(core == 0, angle, pltpu.roll(angle, SLOTS, 1))
        segment = segment_v[...]
        found = jnp.zeros((CHIPS, 128), jnp.int32)
        for s in range(1, SEGS):
            first = jnp.where(segment < s, 1, 0)
            for shift in (1, 2, 4):
                first = first + pltpu.roll(first, shift, 0)
            for shift in (1, 2, 4, 8, 16, 32, 64):
                first = first + pltpu.roll(first, shift, 1)
            found = found + jnp.where(angle >= jnp.concatenate([first, first], axis=0), 1, 0)
        segs_v[...] = found
        pltpu.make_async_copy(segs_v, segs, place_sem.at[0]).start()
        columns = jnp.transpose(angle)
        slots = [jnp.zeros((8, 128), jnp.int32)] * 8
        for c in range(CHIPS):
            for i in range(SLOTS // 8):
                column = jnp.broadcast_to(columns[8 * i : 8 * i + 8, c : c + 1], (8, 128)) - lane
                for b in range(8):
                    slots[b] = jnp.where(column == 128 * b, SLOTS * c + 8 * i + sub, slots[b])
        for b in range(8):
            best = slots[b]
            for shift in (1, 2, 4):
                best = jnp.maximum(best, pltpu.roll(best, shift, 0))
            places_v[b : b + 1, :] = best[:1]
        pltpu.make_async_copy(places_v, places, place_sem.at[1]).start()

    locate()
    take_fields()

    rim = ((sub < 2) & (lane < RIM)) | ((sub >= 6) & (lane >= 128 - RIM))

    pltpu.make_async_copy(segs_v, segs, place_sem.at[0]).wait()

    def absorb(part, accs):
        recv[part, chip] = own[part, chip]
        all_frames(part).wait()

        def batch(i, accs):
            accs = list(accs)
            for u in range(BATCH):
                source = BATCH * i + u
                outer = zero
                for j in range(PAIRS):
                    x = recv[part, source, j].astype(jnp.float32)
                    for f in range(2):
                        k = FRAMES * part + 2 * j + f
                        s = segs[source, k]
                        y = logflat_s[s] - jnp.log(x[8 * f : 8 * f + 8] - dark_s[s])
                        y = y.astype(jnp.bfloat16).astype(jnp.float32)
                        y_v[source * SLOTS + k] = y
                        accs[2 * (u % 2) + f] = accs[2 * (u % 2) + f] + y
                        outer = outer + pltpu.roll(jnp.where(rim, y, zero), 2 * RIM * (2 * j + f), 1)
                edges[part * CHIPS + source] = outer
            return tuple(accs)

        return lax.fori_loop(0, CHIPS // BATCH, batch, accs)

    accs = lax.fori_loop(0, PARTS, absorb, (zero,) * 4)
    for first, count, which in pieces:
        swap(0, first, count, which).wait_send()
    for part in range(1, PARTS):
        swap(part).wait_send()
    pltpu.make_async_copy(places_v, places, place_sem.at[1]).wait()
    profile = ((accs[0] + accs[1]) + (accs[2] + accs[3])) * (1.0 / ANGLES)

    def share(ref, which, t):
        return pltpu.make_async_remote_copy(
            src_ref=ref.at[det],
            dst_ref=ref.at[det],
            send_sem=small_sem.at[which, 0],
            recv_sem=small_sem.at[which, 1],
            device_id=(proj, (det + t) % DET),
            device_id_type=MESH,
        )

    def shared(ref, which):
        others = pl.ds(0, DET - 1)
        return pltpu.make_async_remote_copy(
            src_ref=ref.at[others],
            dst_ref=ref.at[others],
            send_sem=small_sem.at[which, 0],
            recv_sem=small_sem.at[which, 1],
            device_id=(mate, det),
            device_id_type=MESH,
        )

    def arrange(start, stop):
        @pl.loop(start, stop)
        def _(i):
            for u in range(16):
                ordered_out[i * 16 + u] = y_v[places[i // 8, 16 * (i % 8) + u]]

    profs[det] = profile
    for t in (1, 3, 2):
        share(profs, 0, t).start()
    low = jnp.where(sub < 2, zero, pltpu.roll(profile, 2, 0))
    high = jnp.where(sub >= 6, zero, pltpu.roll(profile, 6, 0))
    window = profile
    for o in range(1, RIM + 1):
        window = window + jnp.where(lane >= o, pltpu.roll(profile, o, 1), pltpu.roll(low, o, 1))
        window = window + jnp.where(
            lane < 128 - o, pltpu.roll(profile, 128 - o, 1), pltpu.roll(high, 128 - o, 1)
        )
    column = det * COLS_DEV + (sub // 2) * 128 + lane
    counted = jnp.minimum(column + RIM, COLS - 1) - jnp.maximum(column - RIM, 0) + 1
    counted = counted.astype(jnp.float32)
    inner = profile - window / counted

    def magnitude(i, accs):
        return tuple(
            accs[u] + jnp.abs(y_v[i * 16 + u] - inner) + jnp.abs(y_v[i * 16 + 8 + u] - inner)
            for u in range(8)
        )

    accs = lax.fori_loop(0, ANGLES // 16, magnitude, (zero,) * 8)
    total = ((accs[0] + accs[1]) + (accs[2] + accs[3])) + ((accs[4] + accs[5]) + (accs[6] + accs[7]))
    total = jnp.where(rim, zero, total)
    arrange(0, ARRANGED)
    shared(profs, 0).wait_recv()
    before = pltpu.roll(profs[(det + DET - 1) % DET], 2, 0)
    after = pltpu.roll(profs[(det + 1) % DET], 6, 0)
    before = jnp.where((sub < 2) & (det > 0), before, zero)
    after = jnp.where((sub >= 6) & (det < DET - 1), after, zero)
    for o in range(1, RIM + 1):
        window = window + jnp.where(lane < o, pltpu.roll(before, o, 1), zero)
        window = window + jnp.where(lane >= 128 - o, pltpu.roll(after, 128 - o, 1), zero)
    delta = profile - window / counted
    delta_out[...] = delta

    outer = zero
    for m in range(FRAMES):
        outer = outer + pltpu.roll(jnp.where(rim, delta, zero), 2 * RIM * m, 1)

    def rim_magnitude(i, accs):
        return tuple(accs[u] + jnp.abs(edges[i * 8 + u] - outer) for u in range(8))

    accs = lax.fori_loop(0, PARTS * CHIPS // 8, rim_magnitude, (total,) + (zero,) * 7)
    total = ((accs[0] + accs[1]) + (accs[2] + accs[3])) + ((accs[4] + accs[5]) + (accs[6] + accs[7]))
    sums[det] = total
    for t in (2, 1, 3):
        share(sums, 1, t).start()
    arrange(ARRANGED, ANGLES // 16)
    shared(sums, 1).wait_recv()
    total = (sums[0] + sums[1]) + (sums[2] + sums[3])
    rows = jnp.broadcast_to(jnp.sum(total, axis=1, keepdims=True), (8, 128))
    rows = rows + pltpu.roll(rows, 4, 0)
    rows = rows + pltpu.roll(rows, 2, 0)
    scale = rows * (1.0 / (ANGLES * COLS)) + EPSILON
    bins = jnp.where(
        sub % 2 == 0,
        bin_counts[row_order[2 * proj]],
        bin_counts[row_order[2 * proj + 1]],
    ).astype(jnp.float32)
    factor_out[...] = bins / scale

    for which, ref in enumerate((profs, sums)):
        shared(ref, which).wait_send()


BLOCK = 128
DEPTH = 4


def write_codes(ordered, delta, factor, out, block, sem):
    d, f = delta[...], factor[...]

    def copy(i):
        return pltpu.make_async_copy(
            block.at[i % DEPTH], out.at[pl.ds(i * BLOCK, BLOCK)], sem.at[i % DEPTH]
        )

    @pl.loop(0, ANGLES // BLOCK)
    def _(i):
        @pl.when(i >= DEPTH)
        def _():
            copy(i - DEPTH).wait()

        @pl.loop(0, BLOCK // 16)
        def _(k):
            for u in range(16):
                block[i % DEPTH, k * 16 + u] = (ordered[i * BLOCK + k * 16 + u] - d) * f

        copy(i).start()

    @pl.loop(ANGLES // BLOCK - DEPTH, ANGLES // BLOCK)
    def _(i):
        copy(i).wait()


def on_device(raw, slot_angle, segment_of, seg_owner, flat, dark, row_order, bin_counts):
    vmem = pl.BlockSpec(memory_space=pltpu.VMEM)
    hbm = pl.BlockSpec(memory_space=pltpu.HBM)
    dma = pltpu.SemaphoreType.DMA
    ordered, delta, factor = pl.pallas_call(
        exchange,
        name="exchange",
        out_shape=(
            jax.ShapeDtypeStruct((ANGLES, 8, 128), jnp.float32),
            jax.ShapeDtypeStruct((8, 128), jnp.float32),
            jax.ShapeDtypeStruct((8, 128), jnp.float32),
        ),
        in_specs=[hbm] * 8,
        out_specs=(vmem,) * 3,
        scratch_shapes=[
            pltpu.SMEM((CHIPS, 128), jnp.int32),
            pltpu.SMEM((SEGS,), jnp.int32),
            pltpu.SMEM((ROWS,), jnp.int32),
            pltpu.SMEM((ROWS,), jnp.int32),
            pltpu.VMEM((CHIPS, 128), jnp.int32),
            pltpu.VMEM((8, 128), jnp.int32),
            pltpu.SMEM((CHIPS, 128), jnp.int32),
            pltpu.VMEM((CHIPS, 128), jnp.int32),
            pltpu.SMEM((8, 128), jnp.int32),
            pltpu.VMEM((8, 128), jnp.int32),
            pltpu.VMEM((SLOTS, ROWS, COLS_DEV), jnp.bfloat16),
            pltpu.VMEM((PARTS, CHIPS, PAIRS, 16, 128), jnp.bfloat16),
            pltpu.VMEM((PARTS, CHIPS, PAIRS, 16, 128), jnp.bfloat16),
            pltpu.VMEM((PARTS, CHIPS, PAIRS, 16, 128), jnp.bfloat16),
            pltpu.VMEM((PARTS, CHIPS, PAIRS, 16, 128), jnp.bfloat16),
            pltpu.VMEM((ANGLES, 8, 128), jnp.float32),
            pltpu.VMEM((SEGS, ROWS, COLS_DEV), jnp.float32),
            pltpu.VMEM((SEGS, ROWS, COLS_DEV), jnp.float32),
            pltpu.VMEM((256, 256), jnp.float32),
            pltpu.VMEM((256, 256), jnp.bfloat16),
            pltpu.VMEM((HALVES, RING, RING, HSEGS, 16, 128), jnp.int16),
            pltpu.VMEM((HALVES, RING, RING, HSEGS, 16, 128), jnp.int16),
            pltpu.VMEM((HALVES, RING, RING, HSEGS, 16, 128), jnp.int16),
            pltpu.VMEM((HALVES, RING, RING, HSEGS, 16, 128), jnp.int16),
            pltpu.VMEM((HALVES, RING, HSEGS, 16, 128), jnp.int16),
            pltpu.VMEM((HALVES, RING, HSEGS, 16, 128), jnp.int16),
            pltpu.VMEM((PARTS * CHIPS, 8, 128), jnp.float32),
            pltpu.VMEM((SEGS, 8, 128), jnp.float32),
            pltpu.VMEM((SEGS, 8, 128), jnp.float32),
            pltpu.VMEM((DET, 8, 128), jnp.float32),
            pltpu.VMEM((DET, 8, 128), jnp.float32),
            dma((6,)),
            dma((PARTS,)),
            dma((2,)),
            dma((2,)),
            dma((PARTS + 1,)),
            dma((PARTS + 1,)),
            dma((PARTS,)),
            dma((PARTS,)),
            dma((2,)),
            dma((HALVES, 2)),
            dma((HALVES, 2)),
            dma((2, 2)),
        ],
        compiler_params=pltpu.CompilerParams(
            collective_id=0, has_side_effects=True, vmem_limit_bytes=40 << 20
        ),
    )(
        *(
            pltpu.with_memory_space_constraint(a, pltpu.HBM)
            for a in (
                slot_angle.reshape(CHIPS, 2 * SLOTS),
                segment_of.reshape(8, 128),
                seg_owner,
                row_order,
                bin_counts,
                raw,
                flat,
                dark,
            )
        )
    )
    codes = pl.pallas_call(
        write_codes,
        name="write_codes",
        out_shape=jax.ShapeDtypeStruct((ANGLES, 8, 128), jnp.float32),
        in_specs=[vmem, vmem, vmem],
        out_specs=hbm,
        scratch_shapes=[pltpu.VMEM((DEPTH, BLOCK, 8, 128), jnp.float32), dma((DEPTH,))],
        compiler_params=pltpu.CompilerParams(vmem_limit_bytes=16 << 20),
    )(ordered, delta, factor)
    return codes.reshape(ANGLES, TILES, 2, 128).transpose(0, 2, 1, 3).reshape(ANGLES, 2, COLS_DEV)


def solution(mesh):
    return jax.shard_map(
        on_device,
        mesh=mesh,
        in_specs=(
            P("proj", None, "det"),
            P(),
            P(),
            P(),
            P("proj", None, "det"),
            P("proj", None, "det"),
            P(),
            P(),
        ),
        out_specs=P(None, "proj", "det"),
        check_vma=False,
    )
```

```python
import jax
import jax.numpy as jnp
from jax import lax
from jax.experimental import pallas as pl
from jax.experimental.pallas import tpu as pltpu
from jax.sharding import PartitionSpec as P

MESH = pl.DeviceIdType.MESH

SLOTS = 64
ANGLES = 1024
ROWS = 64
COLS_DEV = 512
COLS = 2048
SEGS = 8
RIM = 8
PROJ = 32
CHIPS = 16
DET = 4
TILES = COLS_DEV // 128
PARTS = 8
FRAMES = SLOTS // PARTS
PAIRS = FRAMES // 2
HEAD = 1
BATCH = 8
ARRANGED = 20
HALVES = 2
RING = 4
HSEGS = SEGS // HALVES
EPSILON = 1e-6
DARK_STEP = 0.2 / 65535.0
FLAT_STEP = 1.0 / 65535.0
STEPS = (
    (2, 2), (1, 2), (2, 1), (3, 2), (2, 3), (1, 1), (3, 3), (1, 3),
    (3, 1), (0, 2), (2, 0), (0, 1), (1, 0), (0, 3), (3, 0),
)


def stack_tiles(frame):
    return jnp.concatenate([frame[:, 128 * t : 128 * (t + 1)] for t in range(TILES)], axis=0)


def coded(field, low, step):
    q = jnp.floor((field - low) * (1.0 / step) + 0.5)
    q = jnp.clip(q, 0.0, 65535.0)
    high = jnp.floor(q * (1.0 / 256.0))
    return high.astype(jnp.bfloat16), (q - 256.0 * high).astype(jnp.bfloat16)


def exchange(
    slot_angle_h,
    segment_of_h,
    seg_owner_h,
    row_order_h,
    bin_counts_h,
    raw,
    flat,
    dark,
    ordered_out,
    delta_out,
    factor_out,
    slot_angle,
    seg_owner,
    row_order,
    bin_counts,
    angle_v,
    segment_v,
    segs,
    segs_v,
    places,
    places_v,
    frames,
    own,
    away,
    mate_in,
    recv,
    y_v,
    flat_v,
    dark_v,
    pick_f,
    pick,
    fsend,
    fmate,
    fpart,
    fring,
    fnext,
    flast,
    edges,
    dark_s,
    logflat_s,
    profs,
    sums,
    int_sem,
    load_sem,
    field_sem,
    place_sem,
    swap_ssem,
    swap_rsem,
    send_sem,
    recv_sem,
    fswap_sem,
    fring_sem,
    flast_sem,
    small_sem,
):
    proj = lax.axis_index("proj")
    det = lax.axis_index("det")
    core = proj % 2
    chip = proj // 2
    col = chip % 4
    lay = chip // 4
    mate = proj + 1 - 2 * core

    def chip_at(step):
        return (lay + step[0]) % 4 * 4 + (col + step[1]) % 4

    barrier = pltpu.get_barrier_semaphore()
    for step in STEPS:
        pl.semaphore_signal(
            barrier, inc=1, device_id=(2 * chip_at(step) + core, det), device_id_type=MESH
        )
    for t in range(1, DET):
        pl.semaphore_signal(
            barrier, inc=1, device_id=(proj, (det + t) % DET), device_id_type=MESH
        )
    pl.semaphore_signal(barrier, inc=1, device_id=(mate, det), device_id_type=MESH)

    ints = []
    for i, (source, target) in enumerate(
        (
            (row_order_h, row_order),
            (slot_angle_h, slot_angle),
            (seg_owner_h, seg_owner),
            (bin_counts_h, bin_counts),
            (slot_angle_h, angle_v),
            (segment_of_h, segment_v),
        )
    ):
        ints.append(pltpu.make_async_copy(source, target, int_sem.at[i]))
        ints[-1].start()
    order = [q for i in range(PARTS // 2) for q in (PARTS - 1 - i, i)]
    loads = {}
    for q in order:
        block = pl.ds(FRAMES * q, FRAMES)
        loads[q] = pltpu.make_async_copy(raw.at[block], frames.at[block], load_sem.at[q])
    flat_copy = pltpu.make_async_copy(flat, flat_v, field_sem.at[0])
    dark_copy = pltpu.make_async_copy(dark, dark_v, field_sem.at[1])

    for q in order[:2]:
        loads[q].start()

    for copy in ints:
        copy.wait()

    sub = lax.broadcasted_iota(jnp.int32, (8, 256), 0)
    lane = lax.broadcasted_iota(jnp.int32, (8, 256), 1)

    @pl.loop(0, PROJ)
    def _(i):
        p = 2 * (i % CHIPS) + (core + i // CHIPS) % 2
        row = jnp.where(sub % 2 == 0, row_order[2 * p], row_order[2 * p + 1])
        hit = lane == row + (sub // 2) * ROWS
        pick_f[pl.ds(pl.multiple_of(8 * i, 8), 8), :] = jnp.where(hit, 1.0, 0.0)

    pick[...] = pick_f[...].astype(jnp.bfloat16)

    def permute(q):
        loads[q].wait()

        @pl.loop(0, PAIRS // 2)
        def _(i):
            block = [stack_tiles(frames[FRAMES * q + 4 * i + f]) for f in range(4)]
            moved = jnp.dot(
                pick[...], jnp.concatenate(block, axis=1), preferred_element_type=jnp.float32
            ).reshape(PROJ, 8, 512)
            part = [moved[:, :, 128 * f : 128 * (f + 1)] for f in range(4)]
            for j in range(2):
                first, second = part[2 * j], part[2 * j + 1]
                own[q, :, 2 * i + j] = jnp.concatenate(
                    [first[:CHIPS], second[:CHIPS]], axis=1
                ).astype(jnp.bfloat16)
                away[PARTS - 1 - q, :, PAIRS - 1 - 2 * i - j] = jnp.concatenate(
                    [second[CHIPS:], first[CHIPS:]], axis=1
                ).astype(jnp.bfloat16)

    def swap(part, first=0, count=PAIRS, which=None):
        which = part if which is None else which
        pairs = pl.ds(first, count)
        return pltpu.make_async_remote_copy(
            src_ref=away.at[part, :, pairs],
            dst_ref=mate_in.at[part, :, pairs],
            send_sem=swap_ssem.at[which],
            recv_sem=swap_rsem.at[which],
            device_id=(mate, det),
            device_id_type=MESH,
        )

    pieces = ((0, HEAD, PARTS), (HEAD, PAIRS - HEAD, 0))

    sub16 = lax.broadcasted_iota(jnp.int32, (16, 128), 0)

    def merge(part, first=0, count=PAIRS):
        @pl.loop(first, first + count)
        def _(j):
            k = SLOTS * core + FRAMES * part + 2 * j
            keep = jnp.where(
                sub16 < 8,
                jnp.where(slot_angle[chip, k] < ANGLES, 1.0, 0.0),
                jnp.where(slot_angle[chip, k + 1] < ANGLES, 1.0, 0.0),
            )
            mine = keep.astype(jnp.bfloat16)
            other = (1.0 - keep).astype(jnp.bfloat16)
            merged = own[part, :, j] * mine + mate_in[part, :, j] * other
            own[part, :, j] = merged

    def frame_copy(part, target, first=0, count=PAIRS):
        pairs = pl.ds(first, count)
        return pltpu.make_async_remote_copy(
            src_ref=own.at[part, target, pairs],
            dst_ref=recv.at[part, chip, pairs],
            send_sem=send_sem.at[part],
            recv_sem=recv_sem.at[part],
            device_id=(2 * target + core, det),
            device_id_type=MESH,
        )

    def ship(part, first=0, count=PAIRS, which=None):
        swap(part, first, count, which).wait_recv()
        merge(part, first, count)
        for step in STEPS:
            frame_copy(part, chip_at(step), first, count).start()

    def all_frames(part):
        chips = pl.ds(0, CHIPS - 1)
        return pltpu.make_async_remote_copy(
            src_ref=own.at[part, chips],
            dst_ref=recv.at[part, chips],
            send_sem=send_sem.at[part],
            recv_sem=recv_sem.at[part],
            device_id=(mate, det),
            device_id_type=MESH,
        )

    def join_copy():
        return pltpu.make_async_remote_copy(
            src_ref=fmate,
            dst_ref=fpart,
            send_sem=fswap_sem.at[0],
            recv_sem=fswap_sem.at[1],
            device_id=(mate, det),
            device_id_type=MESH,
        )

    places_of = ((col, lay), (lay, col))

    def ring_copy(half, d):
        mine = places_of[half][0]
        there = (mine + d) % RING
        target = lay * 4 + there if half == 0 else there * 4 + col
        return pltpu.make_async_remote_copy(
            src_ref=fsend.at[half, there],
            dst_ref=fring.at[half, mine],
            send_sem=fring_sem.at[half, 0],
            recv_sem=fring_sem.at[half, 1],
            device_id=(2 * target + core, det),
            device_id_type=MESH,
        )

    def last_copy(half, d):
        mine = places_of[half][1]
        there = (mine + d) % RING
        target = there * 4 + col if half == 0 else lay * 4 + there
        return pltpu.make_async_remote_copy(
            src_ref=fnext.at[half, there],
            dst_ref=flast.at[half, mine],
            send_sem=flast_sem.at[half, 0],
            recv_sem=flast_sem.at[half, 1],
            device_id=(2 * target + core, det),
            device_id_type=MESH,
        )

    def all_ring(half):
        others = pl.ds(0, RING - 1)
        return pltpu.make_async_remote_copy(
            src_ref=fsend.at[half, others],
            dst_ref=fring.at[half, others],
            send_sem=fring_sem.at[half, 0],
            recv_sem=fring_sem.at[half, 1],
            device_id=(mate, det),
            device_id_type=MESH,
        )

    def all_last(half):
        others = pl.ds(0, RING - 1)
        return pltpu.make_async_remote_copy(
            src_ref=fnext.at[half, others],
            dst_ref=flast.at[half, others],
            send_sem=flast_sem.at[half, 0],
            recv_sem=flast_sem.at[half, 1],
            device_id=(mate, det),
            device_id_type=MESH,
        )

    def code_fields():
        flat_copy.wait()
        dark_copy.wait()
        for half in range(HALVES):

            @pl.loop(0, HSEGS)
            def _(h, half=half):
                s = half * HSEGS + h
                mine = jnp.where(seg_owner[s] == proj, 1.0, 0.0)
                moved = []
                for ref, low, step in ((flat_v, 1.0, FLAT_STEP), (dark_v, 0.0, DARK_STEP)):
                    high, small = coded(stack_tiles(ref[s]), low, step)
                    both = jnp.dot(
                        pick[...],
                        jnp.concatenate([high, small], axis=1),
                        preferred_element_type=jnp.float32,
                    )
                    code = (both[:, :128] * 256.0 + both[:, 128:] - 32768.0) * mine
                    moved.append(code.reshape(PROJ, 8, 128))
                pair = jnp.concatenate(moved, axis=1).astype(jnp.int32).astype(jnp.int16)
                for z in range(RING):
                    for x in range(RING):
                        outer, inner = (x, z) if half == 0 else (z, x)
                        fsend[half, outer, inner, h] = pair[z * RING + x]
                        fmate[half, outer, inner, h] = pair[CHIPS + z * RING + x]

    def ship_fields():
        join_copy().wait()
        for half in range(HALVES):
            mine = places_of[half][0]

            @pl.loop(0, RING)
            def _(o, half=half):
                fsend[half, o] = (
                    fsend[half, o].astype(jnp.int32) + fpart[half, o].astype(jnp.int32)
                ).astype(jnp.int16)

            fring[half, mine] = fsend[half, mine]
        for d in (2, 1, 3):
            for half in range(HALVES):
                ring_copy(half, d).start()

    def pass_fields():
        for half in range(HALVES):
            all_ring(half).wait_recv()
            mine = places_of[half][1]

            @pl.loop(0, RING)
            def _(i, half=half):
                total = fring[half, 0, i].astype(jnp.int32)
                for o in range(1, RING):
                    total = total + fring[half, o, i].astype(jnp.int32)
                fnext[half, i] = total.astype(jnp.int16)

            flast[half, mine] = fnext[half, mine]
            for d in (2, 1, 3):
                last_copy(half, d).start()

    def take_fields():
        for half in range(HALVES):
            all_last(half).wait_recv()
            total = flast[half, 0].astype(jnp.int32)
            for i in range(1, RING):
                total = total + flast[half, i].astype(jnp.int32)
            code = (total + 32768).astype(jnp.float32)
            f = 1.0 + code[:, :8] * FLAT_STEP
            d = code[:, 8:] * DARK_STEP
            dark_s[half * HSEGS : (half + 1) * HSEGS] = d
            logflat_s[half * HSEGS : (half + 1) * HSEGS] = jnp.log(f - d)
            all_ring(half).wait_send()
            all_last(half).wait_send()

    def more(q):
        permute(q)
        swap(PARTS - 1 - q).start()

    for q in order[:2]:
        permute(q)
    for q in order[2:4]:
        loads[q].start()
    flat_copy.start()
    dark_copy.start()
    for q in order[4:]:
        loads[q].start()
    pl.semaphore_wait(barrier, len(STEPS) + DET)
    for first, count, which in pieces:
        swap(0, first, count, which).start()
    swap(PARTS - 1).start()
    for first, count, which in pieces:
        ship(0, first, count, which)
    more(order[2])
    more(order[3])
    code_fields()
    join_copy().start()
    ship(1)
    ship_fields()
    more(order[4])
    more(order[5])
    ship(2)
    more(order[6])
    more(order[7])
    ship(3)
    pass_fields()
    for part in range(4, PARTS):
        ship(part)

    sub = lax.broadcasted_iota(jnp.int32, (8, 128), 0)
    lane = lax.broadcasted_iota(jnp.int32, (8, 128), 1)
    zero = jnp.zeros((8, 128), jnp.float32)

    def locate():
        lane16 = lax.broadcasted_iota(jnp.int32, (CHIPS, 128), 1)
        angle = angle_v[...]
        mirrored = angle
        for bit in (1, 2, 4, 8, 16, 32, 64):
            mirrored = jnp.where(
                lane16 & bit == 0, pltpu.roll(mirrored, 128 - bit, 1), pltpu.roll(mirrored, bit, 1)
            )
        angle = jnp.where(angle < ANGLES, angle, mirrored)
        angle = jnp.where(core == 0, angle, pltpu.roll(angle, SLOTS, 1))
        segment = segment_v[...]
        found = jnp.zeros((CHIPS, 128), jnp.int32)
        for s in range(1, SEGS):
            first = jnp.where(segment < s, 1, 0)
            for shift in (1, 2, 4):
                first = first + pltpu.roll(first, shift, 0)
            for shift in (1, 2, 4, 8, 16, 32, 64):
                first = first + pltpu.roll(first, shift, 1)
            found = found + jnp.where(angle >= jnp.concatenate([first, first], axis=0), 1, 0)
        segs_v[...] = found
        pltpu.make_async_copy(segs_v, segs, place_sem.at[0]).start()
        columns = jnp.transpose(angle)
        slots = [jnp.zeros((8, 128), jnp.int32)] * 8
        for c in range(CHIPS):
            for i in range(SLOTS // 8):
                column = jnp.broadcast_to(columns[8 * i : 8 * i + 8, c : c + 1], (8, 128)) - lane
                for b in range(8):
                    slots[b] = jnp.where(column == 128 * b, SLOTS * c + 8 * i + sub, slots[b])
        for b in range(8):
            best = slots[b]
            for shift in (1, 2, 4):
                best = jnp.maximum(best, pltpu.roll(best, shift, 0))
            places_v[b : b + 1, :] = best[:1]
        pltpu.make_async_copy(places_v, places, place_sem.at[1]).start()

    locate()
    take_fields()

    rim = ((sub < 2) & (lane < RIM)) | ((sub >= 6) & (lane >= 128 - RIM))

    pltpu.make_async_copy(segs_v, segs, place_sem.at[0]).wait()
    for first, count, which in pieces:
        swap(0, first, count, which).wait_send()
    for part in range(1, PARTS):
        swap(part).wait_send()
    pltpu.make_async_copy(places_v, places, place_sem.at[1]).wait()

    def absorb(part, accs):
        recv[part, chip] = own[part, chip]
        all_frames(part).wait()

        def batch(i, accs):
            accs = list(accs)
            for u in range(BATCH):
                source = BATCH * i + u
                outer = zero
                for j in range(PAIRS):
                    x = recv[part, source, j].astype(jnp.float32)
                    for f in range(2):
                        k = FRAMES * part + 2 * j + f
                        s = segs[source, k]
                        y = logflat_s[s] - jnp.log(x[8 * f : 8 * f + 8] - dark_s[s])
                        y = y.astype(jnp.bfloat16).astype(jnp.float32)
                        y_v[source * SLOTS + k] = y
                        accs[2 * (u % 2) + f] = accs[2 * (u % 2) + f] + y
                        outer = outer + pltpu.roll(jnp.where(rim, y, zero), 2 * RIM * (2 * j + f), 1)
                edges[part * CHIPS + source] = outer
            return tuple(accs)

        return lax.fori_loop(0, CHIPS // BATCH, batch, accs)

    accs = lax.fori_loop(0, PARTS, absorb, (zero,) * 4)
    profile = ((accs[0] + accs[1]) + (accs[2] + accs[3])) * (1.0 / ANGLES)

    def share(ref, which, t):
        return pltpu.make_async_remote_copy(
            src_ref=ref.at[det],
            dst_ref=ref.at[det],
            send_sem=small_sem.at[which, 0],
            recv_sem=small_sem.at[which, 1],
            device_id=(proj, (det + t) % DET),
            device_id_type=MESH,
        )

    def shared(ref, which, count):
        others = pl.ds(0, count)
        return pltpu.make_async_remote_copy(
            src_ref=ref.at[others],
            dst_ref=ref.at[others],
            send_sem=small_sem.at[which, 0],
            recv_sem=small_sem.at[which, 1],
            device_id=(mate, det),
            device_id_type=MESH,
        )

    def arrange(start, stop):
        @pl.loop(start, stop)
        def _(i):
            for u in range(16):
                ordered_out[i * 16 + u] = y_v[places[i // 8, 16 * (i % 8) + u]]

    profs[det] = profile
    for t in (1, 3):
        share(profs, 0, t).start()
    low = jnp.where(sub < 2, zero, pltpu.roll(profile, 2, 0))
    high = jnp.where(sub >= 6, zero, pltpu.roll(profile, 6, 0))
    window = profile
    for o in range(1, RIM + 1):
        window = window + jnp.where(lane >= o, pltpu.roll(profile, o, 1), pltpu.roll(low, o, 1))
        window = window + jnp.where(
            lane < 128 - o, pltpu.roll(profile, 128 - o, 1), pltpu.roll(high, 128 - o, 1)
        )
    column = det * COLS_DEV + (sub // 2) * 128 + lane
    counted = jnp.minimum(column + RIM, COLS - 1) - jnp.maximum(column - RIM, 0) + 1
    counted = counted.astype(jnp.float32)
    inner = profile - window / counted

    def magnitude(i, accs):
        return tuple(
            accs[u] + jnp.abs(y_v[i * 16 + u] - inner) + jnp.abs(y_v[i * 16 + 8 + u] - inner)
            for u in range(8)
        )

    accs = lax.fori_loop(0, ANGLES // 16, magnitude, (zero,) * 8)
    total = ((accs[0] + accs[1]) + (accs[2] + accs[3])) + ((accs[4] + accs[5]) + (accs[6] + accs[7]))
    total = jnp.where(rim, zero, total)
    arrange(0, ARRANGED)
    shared(profs, 0, 2).wait_recv()
    before = pltpu.roll(profs[(det + DET - 1) % DET], 2, 0)
    after = pltpu.roll(profs[(det + 1) % DET], 6, 0)
    before = jnp.where((sub < 2) & (det > 0), before, zero)
    after = jnp.where((sub >= 6) & (det < DET - 1), after, zero)
    for o in range(1, RIM + 1):
        window = window + jnp.where(lane < o, pltpu.roll(before, o, 1), zero)
        window = window + jnp.where(lane >= 128 - o, pltpu.roll(after, 128 - o, 1), zero)
    delta = profile - window / counted
    delta_out[...] = delta

    outer = zero
    for m in range(FRAMES):
        outer = outer + pltpu.roll(jnp.where(rim, delta, zero), 2 * RIM * m, 1)

    def rim_magnitude(i, accs):
        return tuple(accs[u] + jnp.abs(edges[i * 8 + u] - outer) for u in range(8))

    accs = lax.fori_loop(0, PARTS * CHIPS // 8, rim_magnitude, (total,) + (zero,) * 7)
    total = ((accs[0] + accs[1]) + (accs[2] + accs[3])) + ((accs[4] + accs[5]) + (accs[6] + accs[7]))
    sums[det] = total
    for t in (2, 1, 3):
        share(sums, 1, t).start()
    arrange(ARRANGED, ANGLES // 16)
    shared(sums, 1, DET - 1).wait_recv()
    total = (sums[0] + sums[1]) + (sums[2] + sums[3])
    rows = jnp.broadcast_to(jnp.sum(total, axis=1, keepdims=True), (8, 128))
    rows = rows + pltpu.roll(rows, 4, 0)
    rows = rows + pltpu.roll(rows, 2, 0)
    scale = rows * (1.0 / (ANGLES * COLS)) + EPSILON
    bins = jnp.where(
        sub % 2 == 0,
        bin_counts[row_order[2 * proj]],
        bin_counts[row_order[2 * proj + 1]],
    ).astype(jnp.float32)
    factor_out[...] = bins / scale

    shared(profs, 0, 2).wait_send()
    shared(sums, 1, DET - 1).wait_send()


BLOCK = 64
DEPTH = 16


def write_codes(ordered, delta, factor, out, block, sem):
    d, f = delta[...], factor[...]

    def copy(i):
        return pltpu.make_async_copy(
            block.at[i % DEPTH], out.at[pl.ds(i * BLOCK, BLOCK)], sem.at[i % DEPTH]
        )

    @pl.loop(0, ANGLES // BLOCK)
    def _(i):
        @pl.when(i >= DEPTH)
        def _():
            copy(i - DEPTH).wait()

        @pl.loop(0, BLOCK // 16)
        def _(k):
            for u in range(16):
                block[i % DEPTH, k * 16 + u] = (ordered[i * BLOCK + k * 16 + u] - d) * f

        copy(i).start()

    @pl.loop(ANGLES // BLOCK - DEPTH, ANGLES // BLOCK)
    def _(i):
        copy(i).wait()


def on_device(raw, slot_angle, segment_of, seg_owner, flat, dark, row_order, bin_counts):
    vmem = pl.BlockSpec(memory_space=pltpu.VMEM)
    hbm = pl.BlockSpec(memory_space=pltpu.HBM)
    dma = pltpu.SemaphoreType.DMA
    ordered, delta, factor = pl.pallas_call(
        exchange,
        name="exchange",
        out_shape=(
            jax.ShapeDtypeStruct((ANGLES, 8, 128), jnp.float32),
            jax.ShapeDtypeStruct((8, 128), jnp.float32),
            jax.ShapeDtypeStruct((8, 128), jnp.float32),
        ),
        in_specs=[hbm] * 8,
        out_specs=(vmem,) * 3,
        scratch_shapes=[
            pltpu.SMEM((CHIPS, 128), jnp.int32),
            pltpu.SMEM((SEGS,), jnp.int32),
            pltpu.SMEM((ROWS,), jnp.int32),
            pltpu.SMEM((ROWS,), jnp.int32),
            pltpu.VMEM((CHIPS, 128), jnp.int32),
            pltpu.VMEM((8, 128), jnp.int32),
            pltpu.SMEM((CHIPS, 128), jnp.int32),
            pltpu.VMEM((CHIPS, 128), jnp.int32),
            pltpu.SMEM((8, 128), jnp.int32),
            pltpu.VMEM((8, 128), jnp.int32),
            pltpu.VMEM((SLOTS, ROWS, COLS_DEV), jnp.bfloat16),
            pltpu.VMEM((PARTS, CHIPS, PAIRS, 16, 128), jnp.bfloat16),
            pltpu.VMEM((PARTS, CHIPS, PAIRS, 16, 128), jnp.bfloat16),
            pltpu.VMEM((PARTS, CHIPS, PAIRS, 16, 128), jnp.bfloat16),
            pltpu.VMEM((PARTS, CHIPS, PAIRS, 16, 128), jnp.bfloat16),
            pltpu.VMEM((ANGLES, 8, 128), jnp.float32),
            pltpu.VMEM((SEGS, ROWS, COLS_DEV), jnp.float32),
            pltpu.VMEM((SEGS, ROWS, COLS_DEV), jnp.float32),
            pltpu.VMEM((256, 256), jnp.float32),
            pltpu.VMEM((256, 256), jnp.bfloat16),
            pltpu.VMEM((HALVES, RING, RING, HSEGS, 16, 128), jnp.int16),
            pltpu.VMEM((HALVES, RING, RING, HSEGS, 16, 128), jnp.int16),
            pltpu.VMEM((HALVES, RING, RING, HSEGS, 16, 128), jnp.int16),
            pltpu.VMEM((HALVES, RING, RING, HSEGS, 16, 128), jnp.int16),
            pltpu.VMEM((HALVES, RING, HSEGS, 16, 128), jnp.int16),
            pltpu.VMEM((HALVES, RING, HSEGS, 16, 128), jnp.int16),
            pltpu.VMEM((PARTS * CHIPS, 8, 128), jnp.float32),
            pltpu.VMEM((SEGS, 8, 128), jnp.float32),
            pltpu.VMEM((SEGS, 8, 128), jnp.float32),
            pltpu.VMEM((DET, 8, 128), jnp.float32),
            pltpu.VMEM((DET, 8, 128), jnp.float32),
            dma((6,)),
            dma((PARTS,)),
            dma((2,)),
            dma((2,)),
            dma((PARTS + 1,)),
            dma((PARTS + 1,)),
            dma((PARTS,)),
            dma((PARTS,)),
            dma((2,)),
            dma((HALVES, 2)),
            dma((HALVES, 2)),
            dma((2, 2)),
        ],
        compiler_params=pltpu.CompilerParams(
            collective_id=0, has_side_effects=True, vmem_limit_bytes=40 << 20
        ),
    )(
        *(
            pltpu.with_memory_space_constraint(a, pltpu.HBM)
            for a in (
                slot_angle.reshape(CHIPS, 2 * SLOTS),
                segment_of.reshape(8, 128),
                seg_owner,
                row_order,
                bin_counts,
                raw,
                flat,
                dark,
            )
        )
    )
    codes = pl.pallas_call(
        write_codes,
        name="write_codes",
        out_shape=jax.ShapeDtypeStruct((ANGLES, 8, 128), jnp.float32),
        in_specs=[vmem, vmem, vmem],
        out_specs=hbm,
        scratch_shapes=[pltpu.VMEM((DEPTH, BLOCK, 8, 128), jnp.float32), dma((DEPTH,))],
        compiler_params=pltpu.CompilerParams(vmem_limit_bytes=16 << 20),
    )(ordered, delta, factor)
    return codes.reshape(ANGLES, TILES, 2, 128).transpose(0, 2, 1, 3).reshape(ANGLES, 2, COLS_DEV)


def solution(mesh):
    return jax.shard_map(
        on_device,
        mesh=mesh,
        in_specs=(
            P("proj", None, "det"),
            P(),
            P(),
            P(),
            P("proj", None, "det"),
            P("proj", None, "det"),
            P(),
            P(),
        ),
        out_specs=P(None, "proj", "det"),
        check_vma=False,
    )
```

```python
import jax
import jax.numpy as jnp
from jax import lax
from jax.experimental import pallas as pl
from jax.experimental.pallas import tpu as pltpu
from jax.sharding import PartitionSpec as P

MESH = pl.DeviceIdType.MESH

SLOTS = 64
ANGLES = 1024
ROWS = 64
COLS_DEV = 512
COLS = 2048
SEGS = 8
RIM = 8
PROJ = 32
CHIPS = 16
DET = 4
TILES = COLS_DEV // 128
PARTS = 8
FRAMES = SLOTS // PARTS
PAIRS = FRAMES // 2
HEAD = 1
LAST = ((0, 7), (7, 15))
BATCH = 8
ARRANGED = 20
HALVES = 2
RING = 4
HSEGS = SEGS // HALVES
EPSILON = 1e-6
DARK_STEP = 0.2 / 65535.0
FLAT_STEP = 1.0 / 65535.0
STEPS = (
    (2, 2), (1, 2), (2, 1), (3, 2), (2, 3), (1, 1), (3, 3), (1, 3),
    (3, 1), (0, 2), (2, 0), (0, 1), (1, 0), (0, 3), (3, 0),
)


def stack_tiles(frame):
    return jnp.concatenate([frame[:, 128 * t : 128 * (t + 1)] for t in range(TILES)], axis=0)


def coded(field, low, step):
    q = jnp.floor((field - low) * (1.0 / step) + 0.5)
    q = jnp.clip(q, 0.0, 65535.0)
    high = jnp.floor(q * (1.0 / 256.0))
    return high.astype(jnp.bfloat16), (q - 256.0 * high).astype(jnp.bfloat16)


def exchange(
    slot_angle_h,
    segment_of_h,
    seg_owner_h,
    row_order_h,
    bin_counts_h,
    raw,
    flat,
    dark,
    ordered_out,
    delta_out,
    factor_out,
    slot_angle,
    seg_owner,
    row_order,
    bin_counts,
    angle_v,
    segment_v,
    segs,
    segs_v,
    places,
    places_v,
    frames,
    own,
    away,
    mate_in,
    recv,
    y_v,
    flat_v,
    dark_v,
    pick_f,
    pick,
    fsend,
    fmate,
    fpart,
    fring,
    fnext,
    flast,
    edges,
    dark_s,
    logflat_s,
    profs,
    sums,
    int_sem,
    load_sem,
    field_sem,
    place_sem,
    swap_ssem,
    swap_rsem,
    send_sem,
    recv_sem,
    fswap_sem,
    fring_sem,
    flast_sem,
    small_sem,
):
    proj = lax.axis_index("proj")
    det = lax.axis_index("det")
    core = proj % 2
    chip = proj // 2
    col = chip % 4
    lay = chip // 4
    mate = proj + 1 - 2 * core

    def chip_at(step):
        return (lay + step[0]) % 4 * 4 + (col + step[1]) % 4

    barrier = pltpu.get_barrier_semaphore()
    for step in STEPS:
        pl.semaphore_signal(
            barrier, inc=1, device_id=(2 * chip_at(step) + core, det), device_id_type=MESH
        )
    for t in range(1, DET):
        pl.semaphore_signal(
            barrier, inc=1, device_id=(proj, (det + t) % DET), device_id_type=MESH
        )
    pl.semaphore_signal(barrier, inc=1, device_id=(mate, det), device_id_type=MESH)

    ints = []
    for i, (source, target) in enumerate(
        (
            (row_order_h, row_order),
            (slot_angle_h, slot_angle),
            (seg_owner_h, seg_owner),
            (bin_counts_h, bin_counts),
            (slot_angle_h, angle_v),
            (segment_of_h, segment_v),
        )
    ):
        ints.append(pltpu.make_async_copy(source, target, int_sem.at[i]))
        ints[-1].start()
    order = [q for i in range(PARTS // 2) for q in (PARTS - 1 - i, i)]
    loads = {}
    for q in order:
        block = pl.ds(FRAMES * q, FRAMES)
        loads[q] = pltpu.make_async_copy(raw.at[block], frames.at[block], load_sem.at[q])
    flat_copy = pltpu.make_async_copy(flat, flat_v, field_sem.at[0])
    dark_copy = pltpu.make_async_copy(dark, dark_v, field_sem.at[1])

    for q in order[:2]:
        loads[q].start()

    for copy in ints:
        copy.wait()

    sub = lax.broadcasted_iota(jnp.int32, (8, 256), 0)
    lane = lax.broadcasted_iota(jnp.int32, (8, 256), 1)

    @pl.loop(0, PROJ)
    def _(i):
        p = 2 * (i % CHIPS) + (core + i // CHIPS) % 2
        row = jnp.where(sub % 2 == 0, row_order[2 * p], row_order[2 * p + 1])
        hit = lane == row + (sub // 2) * ROWS
        pick_f[pl.ds(pl.multiple_of(8 * i, 8), 8), :] = jnp.where(hit, 1.0, 0.0)

    pick[...] = pick_f[...].astype(jnp.bfloat16)

    def permute(q):
        loads[q].wait()

        @pl.loop(0, PAIRS // 2)
        def _(i):
            block = [stack_tiles(frames[FRAMES * q + 4 * i + f]) for f in range(4)]
            moved = jnp.dot(
                pick[...], jnp.concatenate(block, axis=1), preferred_element_type=jnp.float32
            ).reshape(PROJ, 8, 512)
            part = [moved[:, :, 128 * f : 128 * (f + 1)] for f in range(4)]
            for j in range(2):
                first, second = part[2 * j], part[2 * j + 1]
                own[q, :, 2 * i + j] = jnp.concatenate(
                    [first[:CHIPS], second[:CHIPS]], axis=1
                ).astype(jnp.bfloat16)
                away[PARTS - 1 - q, :, PAIRS - 1 - 2 * i - j] = jnp.concatenate(
                    [second[CHIPS:], first[CHIPS:]], axis=1
                ).astype(jnp.bfloat16)

    def swap(part, first=0, count=PAIRS, which=None):
        which = part if which is None else which
        pairs = pl.ds(first, count)
        return pltpu.make_async_remote_copy(
            src_ref=away.at[part, :, pairs],
            dst_ref=mate_in.at[part, :, pairs],
            send_sem=swap_ssem.at[0],
            recv_sem=swap_rsem.at[which],
            device_id=(mate, det),
            device_id_type=MESH,
        )

    pieces = ((0, HEAD, PARTS), (HEAD, PAIRS - HEAD, 0))

    sub16 = lax.broadcasted_iota(jnp.int32, (16, 128), 0)

    def merge(part, first=0, count=PAIRS):
        @pl.loop(first, first + count)
        def _(j):
            k = SLOTS * core + FRAMES * part + 2 * j
            keep = jnp.where(
                sub16 < 8,
                jnp.where(slot_angle[chip, k] < ANGLES, 1.0, 0.0),
                jnp.where(slot_angle[chip, k + 1] < ANGLES, 1.0, 0.0),
            )
            mine = keep.astype(jnp.bfloat16)
            other = (1.0 - keep).astype(jnp.bfloat16)
            merged = own[part, :, j] * mine + mate_in[part, :, j] * other
            own[part, :, j] = merged

    def frame_copy(part, target, first=0, count=PAIRS, sem=None):
        pairs = pl.ds(first, count)
        return pltpu.make_async_remote_copy(
            src_ref=own.at[part, target, pairs],
            dst_ref=recv.at[part, chip, pairs],
            send_sem=send_sem.at[0],
            recv_sem=recv_sem.at[part if sem is None else sem],
            device_id=(2 * target + core, det),
            device_id_type=MESH,
        )

    def ship_last():
        part = PARTS - 1
        swap(part).wait_recv()
        merge(part)
        for i, (first, stop) in enumerate(LAST):
            for step in STEPS[first:stop]:
                frame_copy(part, chip_at(step), sem=part + i).start()

    def ship(part, first=0, count=PAIRS, which=None):
        swap(part, first, count, which).wait_recv()
        merge(part, first, count)
        for step in STEPS:
            frame_copy(part, chip_at(step), first, count).start()

    def last_frames(i):
        chips = pl.ds(0, LAST[i][1] - LAST[i][0])
        return pltpu.make_async_remote_copy(
            src_ref=own.at[PARTS - 1, chips],
            dst_ref=recv.at[PARTS - 1, chips],
            send_sem=send_sem.at[0],
            recv_sem=recv_sem.at[PARTS - 1 + i],
            device_id=(mate, det),
            device_id_type=MESH,
        )

    def all_frames(part):
        chips = pl.ds(0, CHIPS - 1)
        return pltpu.make_async_remote_copy(
            src_ref=own.at[part, chips],
            dst_ref=recv.at[part, chips],
            send_sem=send_sem.at[0],
            recv_sem=recv_sem.at[part],
            device_id=(mate, det),
            device_id_type=MESH,
        )

    def join_copy():
        return pltpu.make_async_remote_copy(
            src_ref=fmate,
            dst_ref=fpart,
            send_sem=fswap_sem.at[0],
            recv_sem=fswap_sem.at[1],
            device_id=(mate, det),
            device_id_type=MESH,
        )

    places_of = ((col, lay), (lay, col))

    def ring_copy(half, d):
        mine = places_of[half][0]
        there = (mine + d) % RING
        target = lay * 4 + there if half == 0 else there * 4 + col
        return pltpu.make_async_remote_copy(
            src_ref=fsend.at[half, there],
            dst_ref=fring.at[half, mine],
            send_sem=fring_sem.at[half, 0],
            recv_sem=fring_sem.at[half, 1],
            device_id=(2 * target + core, det),
            device_id_type=MESH,
        )

    def last_copy(half, d):
        mine = places_of[half][1]
        there = (mine + d) % RING
        target = there * 4 + col if half == 0 else lay * 4 + there
        return pltpu.make_async_remote_copy(
            src_ref=fnext.at[half, there],
            dst_ref=flast.at[half, mine],
            send_sem=flast_sem.at[half, 0],
            recv_sem=flast_sem.at[half, 1],
            device_id=(2 * target + core, det),
            device_id_type=MESH,
        )

    def all_ring(half):
        others = pl.ds(0, RING - 1)
        return pltpu.make_async_remote_copy(
            src_ref=fsend.at[half, others],
            dst_ref=fring.at[half, others],
            send_sem=fring_sem.at[half, 0],
            recv_sem=fring_sem.at[half, 1],
            device_id=(mate, det),
            device_id_type=MESH,
        )

    def all_last(half):
        others = pl.ds(0, RING - 1)
        return pltpu.make_async_remote_copy(
            src_ref=fnext.at[half, others],
            dst_ref=flast.at[half, others],
            send_sem=flast_sem.at[half, 0],
            recv_sem=flast_sem.at[half, 1],
            device_id=(mate, det),
            device_id_type=MESH,
        )

    def code_fields():
        flat_copy.wait()
        dark_copy.wait()
        for half in range(HALVES):

            @pl.loop(0, HSEGS)
            def _(h, half=half):
                s = half * HSEGS + h
                mine = jnp.where(seg_owner[s] == proj, 1.0, 0.0)
                parts = [
                    *coded(stack_tiles(flat_v[s]), 1.0, FLAT_STEP),
                    *coded(stack_tiles(dark_v[s]), 0.0, DARK_STEP),
                ]
                both = jnp.dot(
                    pick[...], jnp.concatenate(parts, axis=1), preferred_element_type=jnp.float32
                )
                moved = []
                for i in (0, 256):
                    code = both[:, i : i + 128] * 256.0 + both[:, i + 128 : i + 256] - 32768.0
                    moved.append((code * mine).reshape(PROJ, 8, 128))
                pair = jnp.concatenate(moved, axis=1).astype(jnp.int32).astype(jnp.int16)
                for z in range(RING):
                    for x in range(RING):
                        outer, inner = (x, z) if half == 0 else (z, x)
                        fsend[half, outer, inner, h] = pair[z * RING + x]
                        fmate[half, outer, inner, h] = pair[CHIPS + z * RING + x]

    def ship_fields():
        join_copy().wait()
        for half in range(HALVES):
            mine = places_of[half][0]

            @pl.loop(0, RING)
            def _(o, half=half):
                fsend[half, o] = (
                    fsend[half, o].astype(jnp.int32) + fpart[half, o].astype(jnp.int32)
                ).astype(jnp.int16)

            fring[half, mine] = fsend[half, mine]
        for d in (2, 1, 3):
            for half in range(HALVES):
                ring_copy(half, d).start()

    def pass_fields():
        for half in range(HALVES):
            all_ring(half).wait_recv()
            mine = places_of[half][1]

            @pl.loop(0, RING)
            def _(i, half=half):
                total = fring[half, 0, i].astype(jnp.int32)
                for o in range(1, RING):
                    total = total + fring[half, o, i].astype(jnp.int32)
                fnext[half, i] = total.astype(jnp.int16)

            flast[half, mine] = fnext[half, mine]
            for d in (2, 1, 3):
                last_copy(half, d).start()

    def take_fields():
        for half in range(HALVES):
            all_last(half).wait_recv()
            total = flast[half, 0].astype(jnp.int32)
            for i in range(1, RING):
                total = total + flast[half, i].astype(jnp.int32)
            code = (total + 32768).astype(jnp.float32)
            f = 1.0 + code[:, :8] * FLAT_STEP
            d = code[:, 8:] * DARK_STEP
            dark_s[half * HSEGS : (half + 1) * HSEGS] = d
            logflat_s[half * HSEGS : (half + 1) * HSEGS] = jnp.log(f - d)
            all_ring(half).wait_send()
            all_last(half).wait_send()

    def more(q):
        permute(q)
        swap(PARTS - 1 - q).start()

    for q in order[:2]:
        permute(q)
    for q in order[2:4]:
        loads[q].start()
    flat_copy.start()
    dark_copy.start()
    for q in order[4:]:
        loads[q].start()
    pl.semaphore_wait(barrier, len(STEPS) + DET)
    for first, count, which in pieces:
        swap(0, first, count, which).start()
    swap(PARTS - 1).start()
    for first, count, which in pieces:
        ship(0, first, count, which)
    more(order[2])
    more(order[3])
    code_fields()
    join_copy().start()
    ship(1)
    more(order[4])
    ship_fields()
    more(order[5])
    ship(2)
    more(order[6])
    more(order[7])
    ship(3)
    pass_fields()
    for part in range(4, PARTS - 1):
        ship(part)
    ship_last()

    sub = lax.broadcasted_iota(jnp.int32, (8, 128), 0)
    lane = lax.broadcasted_iota(jnp.int32, (8, 128), 1)
    zero = jnp.zeros((8, 128), jnp.float32)

    def locate():
        lane16 = lax.broadcasted_iota(jnp.int32, (CHIPS, 128), 1)
        angle = angle_v[...]
        mirrored = angle
        for bit in (1, 2, 4, 8, 16, 32, 64):
            mirrored = jnp.where(
                lane16 & bit == 0, pltpu.roll(mirrored, 128 - bit, 1), pltpu.roll(mirrored, bit, 1)
            )
        angle = jnp.where(angle < ANGLES, angle, mirrored)
        angle = jnp.where(core == 0, angle, pltpu.roll(angle, SLOTS, 1))
        segment = segment_v[...]
        found = jnp.zeros((CHIPS, 128), jnp.int32)
        for s in range(1, SEGS):
            first = jnp.where(segment < s, 1, 0)
            for shift in (1, 2, 4):
                first = first + pltpu.roll(first, shift, 0)
            for shift in (1, 2, 4, 8, 16, 32, 64):
                first = first + pltpu.roll(first, shift, 1)
            found = found + jnp.where(angle >= jnp.concatenate([first, first], axis=0), 1, 0)
        segs_v[...] = found
        pltpu.make_async_copy(segs_v, segs, place_sem.at[0]).start()
        columns = jnp.transpose(angle)
        slots = [jnp.zeros((8, 128), jnp.int32)] * 8
        for c in range(CHIPS):
            for i in range(SLOTS // 8):
                column = jnp.broadcast_to(columns[8 * i : 8 * i + 8, c : c + 1], (8, 128)) - lane
                for b in range(8):
                    slots[b] = jnp.where(column == 128 * b, SLOTS * c + 8 * i + sub, slots[b])
        for b in range(8):
            best = slots[b]
            for shift in (1, 2, 4):
                best = jnp.maximum(best, pltpu.roll(best, shift, 0))
            places_v[b : b + 1, :] = best[:1]
        pltpu.make_async_copy(places_v, places, place_sem.at[1]).start()

    locate()
    take_fields()

    rim = ((sub < 2) & (lane < RIM)) | ((sub >= 6) & (lane >= 128 - RIM))

    pltpu.make_async_copy(segs_v, segs, place_sem.at[0]).wait()
    pltpu.make_async_remote_copy(
        src_ref=away,
        dst_ref=mate_in,
        send_sem=swap_ssem.at[0],
        recv_sem=swap_rsem.at[0],
        device_id=(mate, det),
        device_id_type=MESH,
    ).wait_send()
    pltpu.make_async_copy(places_v, places, place_sem.at[1]).wait()

    def absorb_from(part, sources, accs):
        accs = list(accs)
        for u, source in enumerate(sources):
            outer = zero
            for j in range(PAIRS):
                x = recv[part, source, j].astype(jnp.float32)
                for f in range(2):
                    k = FRAMES * part + 2 * j + f
                    s = segs[source, k]
                    y = logflat_s[s] - jnp.log(x[8 * f : 8 * f + 8] - dark_s[s])
                    y = y.astype(jnp.bfloat16).astype(jnp.float32)
                    y_v[source * SLOTS + k] = y
                    accs[2 * (u % 2) + f] = accs[2 * (u % 2) + f] + y
                    outer = outer + pltpu.roll(jnp.where(rim, y, zero), 2 * RIM * (2 * j + f), 1)
            edges[part * CHIPS + source] = outer
        return tuple(accs)

    def absorb(part, accs):
        recv[part, chip] = own[part, chip]
        all_frames(part).wait_recv()

        def batch(i, accs):
            return absorb_from(part, [BATCH * i + u for u in range(BATCH)], accs)

        return lax.fori_loop(0, CHIPS // BATCH, batch, accs)

    accs = lax.fori_loop(0, PARTS - 1, absorb, (zero,) * 4)
    recv[PARTS - 1, chip] = own[PARTS - 1, chip]
    for i, (first, stop) in enumerate(LAST):
        last_frames(i).wait_recv()
        sources = [chip_at((4 - step[0], 4 - step[1])) for step in STEPS[first:stop]]
        accs = absorb_from(PARTS - 1, sources + ([chip] if i == 0 else []), accs)
    profile = ((accs[0] + accs[1]) + (accs[2] + accs[3])) * (1.0 / ANGLES)

    def share(ref, which, t):
        return pltpu.make_async_remote_copy(
            src_ref=ref.at[det],
            dst_ref=ref.at[det],
            send_sem=small_sem.at[which, 0],
            recv_sem=small_sem.at[which, 1],
            device_id=(proj, (det + t) % DET),
            device_id_type=MESH,
        )

    def shared(ref, which, count):
        others = pl.ds(0, count)
        return pltpu.make_async_remote_copy(
            src_ref=ref.at[others],
            dst_ref=ref.at[others],
            send_sem=small_sem.at[which, 0],
            recv_sem=small_sem.at[which, 1],
            device_id=(mate, det),
            device_id_type=MESH,
        )

    def arrange(start, stop):
        @pl.loop(start, stop)
        def _(i):
            for u in range(16):
                ordered_out[i * 16 + u] = y_v[places[i // 8, 16 * (i % 8) + u]]

    profs[det] = profile
    for t in (1, 3):
        share(profs, 0, t).start()
    low = jnp.where(sub < 2, zero, pltpu.roll(profile, 2, 0))
    high = jnp.where(sub >= 6, zero, pltpu.roll(profile, 6, 0))
    window = profile
    for o in range(1, RIM + 1):
        window = window + jnp.where(lane >= o, pltpu.roll(profile, o, 1), pltpu.roll(low, o, 1))
        window = window + jnp.where(
            lane < 128 - o, pltpu.roll(profile, 128 - o, 1), pltpu.roll(high, 128 - o, 1)
        )
    column = det * COLS_DEV + (sub // 2) * 128 + lane
    counted = jnp.minimum(column + RIM, COLS - 1) - jnp.maximum(column - RIM, 0) + 1
    counted = counted.astype(jnp.float32)
    inner = profile - window / counted

    def magnitude(i, accs):
        return tuple(
            accs[u] + jnp.abs(y_v[i * 16 + u] - inner) + jnp.abs(y_v[i * 16 + 8 + u] - inner)
            for u in range(8)
        )

    accs = lax.fori_loop(0, ANGLES // 16, magnitude, (zero,) * 8)
    total = ((accs[0] + accs[1]) + (accs[2] + accs[3])) + ((accs[4] + accs[5]) + (accs[6] + accs[7]))
    total = jnp.where(rim, zero, total)
    arrange(0, ARRANGED)
    shared(profs, 0, 2).wait_recv()
    before = pltpu.roll(profs[(det + DET - 1) % DET], 2, 0)
    after = pltpu.roll(profs[(det + 1) % DET], 6, 0)
    before = jnp.where((sub < 2) & (det > 0), before, zero)
    after = jnp.where((sub >= 6) & (det < DET - 1), after, zero)
    for o in range(1, RIM + 1):
        window = window + jnp.where(lane < o, pltpu.roll(before, o, 1), zero)
        window = window + jnp.where(lane >= 128 - o, pltpu.roll(after, 128 - o, 1), zero)
    delta = profile - window / counted
    delta_out[...] = delta

    outer = zero
    for m in range(FRAMES):
        outer = outer + pltpu.roll(jnp.where(rim, delta, zero), 2 * RIM * m, 1)

    def rim_magnitude(i, accs):
        return tuple(accs[u] + jnp.abs(edges[i * 8 + u] - outer) for u in range(8))

    accs = lax.fori_loop(0, PARTS * CHIPS // 8, rim_magnitude, (total,) + (zero,) * 7)
    total = ((accs[0] + accs[1]) + (accs[2] + accs[3])) + ((accs[4] + accs[5]) + (accs[6] + accs[7]))
    sums[det] = total
    for t in (2, 1, 3):
        share(sums, 1, t).start()
    arrange(ARRANGED, ANGLES // 16)
    shared(sums, 1, DET - 1).wait_recv()
    total = (sums[0] + sums[1]) + (sums[2] + sums[3])
    rows = jnp.broadcast_to(jnp.sum(total, axis=1, keepdims=True), (8, 128))
    rows = rows + pltpu.roll(rows, 4, 0)
    rows = rows + pltpu.roll(rows, 2, 0)
    scale = rows * (1.0 / (ANGLES * COLS)) + EPSILON
    bins = jnp.where(
        sub % 2 == 0,
        bin_counts[row_order[2 * proj]],
        bin_counts[row_order[2 * proj + 1]],
    ).astype(jnp.float32)
    factor_out[...] = bins / scale

    every = (pl.ds(0, PARTS), pl.ds(0, CHIPS - 1))
    pltpu.make_async_remote_copy(
        src_ref=own.at[every],
        dst_ref=recv.at[every],
        send_sem=send_sem.at[0],
        recv_sem=recv_sem.at[0],
        device_id=(mate, det),
        device_id_type=MESH,
    ).wait_send()
    shared(profs, 0, 2).wait_send()
    shared(sums, 1, DET - 1).wait_send()


BLOCK = 64
DEPTH = 16


def write_codes(ordered, delta, factor, out, block, sem):
    d, f = delta[...], factor[...]

    def copy(i):
        return pltpu.make_async_copy(
            block.at[i % DEPTH], out.at[pl.ds(i * BLOCK, BLOCK)], sem.at[i % DEPTH]
        )

    @pl.loop(0, ANGLES // BLOCK)
    def _(i):
        @pl.when(i >= DEPTH)
        def _():
            copy(i - DEPTH).wait()

        @pl.loop(0, BLOCK // 16)
        def _(k):
            for u in range(16):
                block[i % DEPTH, k * 16 + u] = (ordered[i * BLOCK + k * 16 + u] - d) * f

        copy(i).start()

    @pl.loop(ANGLES // BLOCK - DEPTH, ANGLES // BLOCK)
    def _(i):
        copy(i).wait()


def on_device(raw, slot_angle, segment_of, seg_owner, flat, dark, row_order, bin_counts):
    vmem = pl.BlockSpec(memory_space=pltpu.VMEM)
    hbm = pl.BlockSpec(memory_space=pltpu.HBM)
    dma = pltpu.SemaphoreType.DMA
    ordered, delta, factor = pl.pallas_call(
        exchange,
        name="exchange",
        out_shape=(
            jax.ShapeDtypeStruct((ANGLES, 8, 128), jnp.float32),
            jax.ShapeDtypeStruct((8, 128), jnp.float32),
            jax.ShapeDtypeStruct((8, 128), jnp.float32),
        ),
        in_specs=[hbm] * 8,
        out_specs=(vmem,) * 3,
        scratch_shapes=[
            pltpu.SMEM((CHIPS, 128), jnp.int32),
            pltpu.SMEM((SEGS,), jnp.int32),
            pltpu.SMEM((ROWS,), jnp.int32),
            pltpu.SMEM((ROWS,), jnp.int32),
            pltpu.VMEM((CHIPS, 128), jnp.int32),
            pltpu.VMEM((8, 128), jnp.int32),
            pltpu.SMEM((CHIPS, 128), jnp.int32),
            pltpu.VMEM((CHIPS, 128), jnp.int32),
            pltpu.SMEM((8, 128), jnp.int32),
            pltpu.VMEM((8, 128), jnp.int32),
            pltpu.VMEM((SLOTS, ROWS, COLS_DEV), jnp.bfloat16),
            pltpu.VMEM((PARTS, CHIPS, PAIRS, 16, 128), jnp.bfloat16),
            pltpu.VMEM((PARTS, CHIPS, PAIRS, 16, 128), jnp.bfloat16),
            pltpu.VMEM((PARTS, CHIPS, PAIRS, 16, 128), jnp.bfloat16),
            pltpu.VMEM((PARTS, CHIPS, PAIRS, 16, 128), jnp.bfloat16),
            pltpu.VMEM((ANGLES, 8, 128), jnp.float32),
            pltpu.VMEM((SEGS, ROWS, COLS_DEV), jnp.float32),
            pltpu.VMEM((SEGS, ROWS, COLS_DEV), jnp.float32),
            pltpu.VMEM((256, 256), jnp.float32),
            pltpu.VMEM((256, 256), jnp.bfloat16),
            pltpu.VMEM((HALVES, RING, RING, HSEGS, 16, 128), jnp.int16),
            pltpu.VMEM((HALVES, RING, RING, HSEGS, 16, 128), jnp.int16),
            pltpu.VMEM((HALVES, RING, RING, HSEGS, 16, 128), jnp.int16),
            pltpu.VMEM((HALVES, RING, RING, HSEGS, 16, 128), jnp.int16),
            pltpu.VMEM((HALVES, RING, HSEGS, 16, 128), jnp.int16),
            pltpu.VMEM((HALVES, RING, HSEGS, 16, 128), jnp.int16),
            pltpu.VMEM((PARTS * CHIPS, 8, 128), jnp.float32),
            pltpu.VMEM((SEGS, 8, 128), jnp.float32),
            pltpu.VMEM((SEGS, 8, 128), jnp.float32),
            pltpu.VMEM((DET, 8, 128), jnp.float32),
            pltpu.VMEM((DET, 8, 128), jnp.float32),
            dma((6,)),
            dma((PARTS,)),
            dma((2,)),
            dma((2,)),
            dma((1,)),
            dma((PARTS + 1,)),
            dma((1,)),
            dma((PARTS - 1 + len(LAST),)),
            dma((2,)),
            dma((HALVES, 2)),
            dma((HALVES, 2)),
            dma((2, 2)),
        ],
        compiler_params=pltpu.CompilerParams(
            collective_id=0, has_side_effects=True, vmem_limit_bytes=40 << 20
        ),
    )(
        *(
            pltpu.with_memory_space_constraint(a, pltpu.HBM)
            for a in (
                slot_angle.reshape(CHIPS, 2 * SLOTS),
                segment_of.reshape(8, 128),
                seg_owner,
                row_order,
                bin_counts,
                raw,
                flat,
                dark,
            )
        )
    )
    codes = pl.pallas_call(
        write_codes,
        name="write_codes",
        out_shape=jax.ShapeDtypeStruct((ANGLES, 8, 128), jnp.float32),
        in_specs=[vmem, vmem, vmem],
        out_specs=hbm,
        scratch_shapes=[pltpu.VMEM((DEPTH, BLOCK, 8, 128), jnp.float32), dma((DEPTH,))],
        compiler_params=pltpu.CompilerParams(vmem_limit_bytes=16 << 20),
    )(ordered, delta, factor)
    return codes.reshape(ANGLES, TILES, 2, 128).transpose(0, 2, 1, 3).reshape(ANGLES, 2, COLS_DEV)


def solution(mesh):
    return jax.shard_map(
        on_device,
        mesh=mesh,
        in_specs=(
            P("proj", None, "det"),
            P(),
            P(),
            P(),
            P("proj", None, "det"),
            P("proj", None, "det"),
            P(),
            P(),
        ),
        out_specs=P(None, "proj", "det"),
        check_vma=False,
    )
```

```python
import jax
import jax.numpy as jnp
from jax import lax
from jax.experimental import pallas as pl
from jax.experimental.pallas import tpu as pltpu
from jax.sharding import PartitionSpec as P

MESH = pl.DeviceIdType.MESH

SLOTS = 64
ANGLES = 1024
ROWS = 64
COLS_DEV = 512
COLS = 2048
SEGS = 8
RIM = 8
PROJ = 32
CHIPS = 16
DET = 4
TILES = COLS_DEV // 128
PARTS = 8
FRAMES = SLOTS // PARTS
PAIRS = FRAMES // 2
HEAD = 1
LAST = ((0, 7), (7, 15))
BATCH = 8
ARRANGED = 20
HALVES = 2
RING = 4
HSEGS = SEGS // HALVES
EPSILON = 1e-6
DARK_STEP = 0.2 / 65535.0
FLAT_STEP = 1.0 / 65535.0
STEPS = (
    (2, 2), (1, 2), (2, 1), (3, 2), (2, 3), (1, 1), (3, 3), (1, 3),
    (3, 1), (0, 2), (2, 0), (0, 1), (1, 0), (0, 3), (3, 0),
)


def stack_tiles(frame):
    return jnp.concatenate([frame[:, 128 * t : 128 * (t + 1)] for t in range(TILES)], axis=0)


def coded(field, low, step):
    q = jnp.floor((field - low) * (1.0 / step) + 0.5)
    q = jnp.clip(q, 0.0, 65535.0)
    high = jnp.floor(q * (1.0 / 256.0))
    return high.astype(jnp.bfloat16), (q - 256.0 * high).astype(jnp.bfloat16)


def exchange(
    slot_angle_h,
    segment_of_h,
    seg_owner_h,
    row_order_h,
    bin_counts_h,
    raw,
    flat,
    dark,
    ordered_out,
    delta_out,
    factor_out,
    slot_angle,
    seg_owner,
    row_order,
    bin_counts,
    angle_v,
    segment_v,
    segs,
    segs_v,
    places,
    places_v,
    frames,
    own,
    away,
    mate_in,
    recv,
    y_v,
    flat_v,
    dark_v,
    pick_f,
    pick,
    fsend,
    fmate,
    fpart,
    fring,
    fnext,
    flast,
    edges,
    dark_s,
    logflat_s,
    profs,
    sums,
    int_sem,
    load_sem,
    field_sem,
    place_sem,
    swap_ssem,
    swap_rsem,
    send_sem,
    recv_sem,
    fswap_sem,
    fring_sem,
    flast_sem,
    small_sem,
):
    proj = lax.axis_index("proj")
    det = lax.axis_index("det")
    core = proj % 2
    chip = proj // 2
    col = chip % 4
    lay = chip // 4
    mate = proj + 1 - 2 * core

    def chip_at(step):
        return (lay + step[0]) % 4 * 4 + (col + step[1]) % 4

    barrier = pltpu.get_barrier_semaphore()
    for step in STEPS:
        pl.semaphore_signal(
            barrier, inc=1, device_id=(2 * chip_at(step) + core, det), device_id_type=MESH
        )
    for t in range(1, DET):
        pl.semaphore_signal(
            barrier, inc=1, device_id=(proj, (det + t) % DET), device_id_type=MESH
        )
    pl.semaphore_signal(barrier, inc=1, device_id=(mate, det), device_id_type=MESH)

    ints = []
    for i, (source, target) in enumerate(
        (
            (row_order_h, row_order),
            (slot_angle_h, slot_angle),
            (seg_owner_h, seg_owner),
            (bin_counts_h, bin_counts),
            (slot_angle_h, angle_v),
            (segment_of_h, segment_v),
        )
    ):
        ints.append(pltpu.make_async_copy(source, target, int_sem.at[i]))
        ints[-1].start()
    order = [q for i in range(PARTS // 2) for q in (PARTS - 1 - i, i)]
    loads = {}
    for q in order:
        block = pl.ds(FRAMES * q, FRAMES)
        loads[q] = pltpu.make_async_copy(raw.at[block], frames.at[block], load_sem.at[q])
    flat_copy = pltpu.make_async_copy(flat, flat_v, field_sem.at[0])
    dark_copy = pltpu.make_async_copy(dark, dark_v, field_sem.at[1])

    for q in order[:2]:
        loads[q].start()

    for copy in ints:
        copy.wait()

    sub = lax.broadcasted_iota(jnp.int32, (8, 256), 0)
    lane = lax.broadcasted_iota(jnp.int32, (8, 256), 1)

    @pl.loop(0, PROJ)
    def _(i):
        p = 2 * (i % CHIPS) + (core + i // CHIPS) % 2
        row = jnp.where(sub % 2 == 0, row_order[2 * p], row_order[2 * p + 1])
        hit = lane == row + (sub // 2) * ROWS
        pick_f[pl.ds(pl.multiple_of(8 * i, 8), 8), :] = jnp.where(hit, 1.0, 0.0)

    pick[...] = pick_f[...].astype(jnp.bfloat16)

    def permute(q):
        loads[q].wait()

        @pl.loop(0, PAIRS // 2)
        def _(i):
            block = [stack_tiles(frames[FRAMES * q + 4 * i + f]) for f in range(4)]
            moved = jnp.dot(
                pick[...], jnp.concatenate(block, axis=1), preferred_element_type=jnp.float32
            ).reshape(PROJ, 8, 512)
            part = [moved[:, :, 128 * f : 128 * (f + 1)] for f in range(4)]
            for j in range(2):
                first, second = part[2 * j], part[2 * j + 1]
                own[q, :, 2 * i + j] = jnp.concatenate(
                    [first[:CHIPS], second[:CHIPS]], axis=1
                ).astype(jnp.bfloat16)
                away[PARTS - 1 - q, :, PAIRS - 1 - 2 * i - j] = jnp.concatenate(
                    [second[CHIPS:], first[CHIPS:]], axis=1
                ).astype(jnp.bfloat16)

    def swap(part, first=0, count=PAIRS, which=None):
        which = part if which is None else which
        pairs = pl.ds(first, count)
        return pltpu.make_async_remote_copy(
            src_ref=away.at[part, :, pairs],
            dst_ref=mate_in.at[part, :, pairs],
            send_sem=swap_ssem.at[0],
            recv_sem=swap_rsem.at[which],
            device_id=(mate, det),
            device_id_type=MESH,
        )

    pieces = ((0, HEAD, PARTS), (HEAD, PAIRS - HEAD, 0))

    sub16 = lax.broadcasted_iota(jnp.int32, (16, 128), 0)

    def merge(part, first=0, count=PAIRS):
        @pl.loop(first, first + count)
        def _(j):
            k = SLOTS * core + FRAMES * part + 2 * j
            keep = jnp.where(
                sub16 < 8,
                jnp.where(slot_angle[chip, k] < ANGLES, 1.0, 0.0),
                jnp.where(slot_angle[chip, k + 1] < ANGLES, 1.0, 0.0),
            )
            mine = keep.astype(jnp.bfloat16)
            other = (1.0 - keep).astype(jnp.bfloat16)
            merged = own[part, :, j] * mine + mate_in[part, :, j] * other
            own[part, :, j] = merged

    def frame_copy(part, target, first=0, count=PAIRS, sem=None):
        pairs = pl.ds(first, count)
        return pltpu.make_async_remote_copy(
            src_ref=own.at[part, target, pairs],
            dst_ref=recv.at[part, chip, pairs],
            send_sem=send_sem.at[0],
            recv_sem=recv_sem.at[part if sem is None else sem],
            device_id=(2 * target + core, det),
            device_id_type=MESH,
        )

    def ship_last():
        part = PARTS - 1
        swap(part).wait_recv()
        merge(part)
        for i, (first, stop) in enumerate(LAST):
            for step in STEPS[first:stop]:
                frame_copy(part, chip_at(step), sem=part + i).start()

    def ship(part, first=0, count=PAIRS, which=None):
        swap(part, first, count, which).wait_recv()
        merge(part, first, count)
        for step in STEPS:
            frame_copy(part, chip_at(step), first, count).start()

    def last_frames(i):
        chips = pl.ds(0, LAST[i][1] - LAST[i][0])
        return pltpu.make_async_remote_copy(
            src_ref=own.at[PARTS - 1, chips],
            dst_ref=recv.at[PARTS - 1, chips],
            send_sem=send_sem.at[0],
            recv_sem=recv_sem.at[PARTS - 1 + i],
            device_id=(mate, det),
            device_id_type=MESH,
        )

    def all_frames(part):
        chips = pl.ds(0, CHIPS - 1)
        return pltpu.make_async_remote_copy(
            src_ref=own.at[part, chips],
            dst_ref=recv.at[part, chips],
            send_sem=send_sem.at[0],
            recv_sem=recv_sem.at[part],
            device_id=(mate, det),
            device_id_type=MESH,
        )

    def join_copy():
        return pltpu.make_async_remote_copy(
            src_ref=fmate,
            dst_ref=fpart,
            send_sem=fswap_sem.at[0],
            recv_sem=fswap_sem.at[1],
            device_id=(mate, det),
            device_id_type=MESH,
        )

    places_of = ((col, lay), (lay, col))

    def ring_copy(half, d):
        mine = places_of[half][0]
        there = (mine + d) % RING
        target = lay * 4 + there if half == 0 else there * 4 + col
        return pltpu.make_async_remote_copy(
            src_ref=fsend.at[half, there],
            dst_ref=fring.at[half, mine],
            send_sem=fring_sem.at[half, 0],
            recv_sem=fring_sem.at[half, 1],
            device_id=(2 * target + core, det),
            device_id_type=MESH,
        )

    def last_copy(half, d):
        mine = places_of[half][1]
        there = (mine + d) % RING
        target = there * 4 + col if half == 0 else lay * 4 + there
        return pltpu.make_async_remote_copy(
            src_ref=fnext.at[half, there],
            dst_ref=flast.at[half, mine],
            send_sem=flast_sem.at[half, 0],
            recv_sem=flast_sem.at[half, 1],
            device_id=(2 * target + core, det),
            device_id_type=MESH,
        )

    def all_ring(half):
        others = pl.ds(0, RING - 1)
        return pltpu.make_async_remote_copy(
            src_ref=fsend.at[half, others],
            dst_ref=fring.at[half, others],
            send_sem=fring_sem.at[half, 0],
            recv_sem=fring_sem.at[half, 1],
            device_id=(mate, det),
            device_id_type=MESH,
        )

    def all_last(half):
        others = pl.ds(0, RING - 1)
        return pltpu.make_async_remote_copy(
            src_ref=fnext.at[half, others],
            dst_ref=flast.at[half, others],
            send_sem=flast_sem.at[half, 0],
            recv_sem=flast_sem.at[half, 1],
            device_id=(mate, det),
            device_id_type=MESH,
        )

    def code_fields():
        flat_copy.wait()
        dark_copy.wait()
        for half in range(HALVES):

            @pl.loop(0, HSEGS)
            def _(h, half=half):
                s = half * HSEGS + h
                mine = jnp.where(seg_owner[s] == proj, 1.0, 0.0)
                parts = [
                    *coded(stack_tiles(flat_v[s]), 1.0, FLAT_STEP),
                    *coded(stack_tiles(dark_v[s]), 0.0, DARK_STEP),
                ]
                both = jnp.dot(
                    pick[...], jnp.concatenate(parts, axis=1), preferred_element_type=jnp.float32
                )
                moved = []
                for i in (0, 256):
                    code = both[:, i : i + 128] * 256.0 + both[:, i + 128 : i + 256] - 32768.0
                    moved.append((code * mine).reshape(PROJ, 8, 128))
                pair = jnp.concatenate(moved, axis=1).astype(jnp.int32).astype(jnp.int16)
                for z in range(RING):
                    for x in range(RING):
                        outer, inner = (x, z) if half == 0 else (z, x)
                        fsend[half, outer, inner, h] = pair[z * RING + x]
                        fmate[half, outer, inner, h] = pair[CHIPS + z * RING + x]

    def ship_fields():
        join_copy().wait()
        for half in range(HALVES):
            mine = places_of[half][0]

            @pl.loop(0, RING)
            def _(o, half=half):
                fsend[half, o] = (
                    fsend[half, o].astype(jnp.int32) + fpart[half, o].astype(jnp.int32)
                ).astype(jnp.int16)

            fring[half, mine] = fsend[half, mine]
        for d in (2, 1, 3):
            for half in range(HALVES):
                ring_copy(half, d).start()

    def pass_fields():
        for half in range(HALVES):
            all_ring(half).wait_recv()
            mine = places_of[half][1]

            @pl.loop(0, RING)
            def _(i, half=half):
                total = fring[half, 0, i].astype(jnp.int32)
                for o in range(1, RING):
                    total = total + fring[half, o, i].astype(jnp.int32)
                fnext[half, i] = total.astype(jnp.int16)

            flast[half, mine] = fnext[half, mine]
            for d in (2, 1, 3):
                last_copy(half, d).start()

    def take_fields():
        for half in range(HALVES):
            all_last(half).wait_recv()
            total = flast[half, 0].astype(jnp.int32)
            for i in range(1, RING):
                total = total + flast[half, i].astype(jnp.int32)
            code = (total + 32768).astype(jnp.float32)
            f = 1.0 + code[:, :8] * FLAT_STEP
            d = code[:, 8:] * DARK_STEP
            dark_s[half * HSEGS : (half + 1) * HSEGS] = d
            logflat_s[half * HSEGS : (half + 1) * HSEGS] = jnp.log(f - d)
            all_ring(half).wait_send()
            all_last(half).wait_send()

    def more(q):
        permute(q)
        swap(PARTS - 1 - q).start()

    for q in order[:2]:
        permute(q)
    for q in order[2:4]:
        loads[q].start()
    flat_copy.start()
    dark_copy.start()
    for q in order[4:]:
        loads[q].start()
    pl.semaphore_wait(barrier, len(STEPS) + DET)
    for first, count, which in pieces:
        swap(0, first, count, which).start()
    for first, count, which in pieces:
        ship(0, first, count, which)
    more(order[2])
    permute(order[3])
    code_fields()
    join_copy().start()
    ship(1)
    more(order[4])
    ship_fields()
    permute(order[5])
    ship(2)
    for q in (order[1], order[3], order[5]):
        swap(PARTS - 1 - q).start()
    more(order[6])
    more(order[7])
    ship(3)
    pass_fields()
    for part in range(4, PARTS - 1):
        ship(part)
    ship_last()

    sub = lax.broadcasted_iota(jnp.int32, (8, 128), 0)
    lane = lax.broadcasted_iota(jnp.int32, (8, 128), 1)
    zero = jnp.zeros((8, 128), jnp.float32)

    def locate():
        lane16 = lax.broadcasted_iota(jnp.int32, (CHIPS, 128), 1)
        angle = angle_v[...]
        mirrored = angle
        for bit in (1, 2, 4, 8, 16, 32, 64):
            mirrored = jnp.where(
                lane16 & bit == 0, pltpu.roll(mirrored, 128 - bit, 1), pltpu.roll(mirrored, bit, 1)
            )
        angle = jnp.where(angle < ANGLES, angle, mirrored)
        angle = jnp.where(core == 0, angle, pltpu.roll(angle, SLOTS, 1))
        segment = segment_v[...]
        found = jnp.zeros((CHIPS, 128), jnp.int32)
        for s in range(1, SEGS):
            first = jnp.where(segment < s, 1, 0)
            for shift in (1, 2, 4):
                first = first + pltpu.roll(first, shift, 0)
            for shift in (1, 2, 4, 8, 16, 32, 64):
                first = first + pltpu.roll(first, shift, 1)
            found = found + jnp.where(angle >= jnp.concatenate([first, first], axis=0), 1, 0)
        segs_v[...] = found
        pltpu.make_async_copy(segs_v, segs, place_sem.at[0]).start()
        columns = jnp.transpose(angle)
        slots = [jnp.zeros((8, 128), jnp.int32)] * 8
        for c in range(CHIPS):
            for i in range(SLOTS // 8):
                column = jnp.broadcast_to(columns[8 * i : 8 * i + 8, c : c + 1], (8, 128)) - lane
                for b in range(8):
                    slots[b] = jnp.where(column == 128 * b, SLOTS * c + 8 * i + sub, slots[b])
        for b in range(8):
            best = slots[b]
            for shift in (1, 2, 4):
                best = jnp.maximum(best, pltpu.roll(best, shift, 0))
            places_v[b : b + 1, :] = best[:1]
        pltpu.make_async_copy(places_v, places, place_sem.at[1]).start()

    locate()
    take_fields()

    rim = ((sub < 2) & (lane < RIM)) | ((sub >= 6) & (lane >= 128 - RIM))

    pltpu.make_async_copy(segs_v, segs, place_sem.at[0]).wait()
    pltpu.make_async_remote_copy(
        src_ref=away,
        dst_ref=mate_in,
        send_sem=swap_ssem.at[0],
        recv_sem=swap_rsem.at[0],
        device_id=(mate, det),
        device_id_type=MESH,
    ).wait_send()
    pltpu.make_async_copy(places_v, places, place_sem.at[1]).wait()

    def absorb_from(part, sources, accs):
        accs = list(accs)
        for u, source in enumerate(sources):
            outer = zero
            for j in range(PAIRS):
                x = recv[part, source, j].astype(jnp.float32)
                for f in range(2):
                    k = FRAMES * part + 2 * j + f
                    s = segs[source, k]
                    y = logflat_s[s] - jnp.log(x[8 * f : 8 * f + 8] - dark_s[s])
                    y = y.astype(jnp.bfloat16).astype(jnp.float32)
                    y_v[source * SLOTS + k] = y
                    accs[2 * (u % 2) + f] = accs[2 * (u % 2) + f] + y
                    outer = outer + pltpu.roll(jnp.where(rim, y, zero), 2 * RIM * (2 * j + f), 1)
            edges[part * CHIPS + source] = outer
        return tuple(accs)

    def absorb(part, accs):
        recv[part, chip] = own[part, chip]
        all_frames(part).wait_recv()

        def batch(i, accs):
            return absorb_from(part, [BATCH * i + u for u in range(BATCH)], accs)

        return lax.fori_loop(0, CHIPS // BATCH, batch, accs)

    accs = lax.fori_loop(0, PARTS - 1, absorb, (zero,) * 4)
    recv[PARTS - 1, chip] = own[PARTS - 1, chip]
    for i, (first, stop) in enumerate(LAST):
        last_frames(i).wait_recv()
        sources = [chip_at((4 - step[0], 4 - step[1])) for step in STEPS[first:stop]]
        accs = absorb_from(PARTS - 1, sources + ([chip] if i == 0 else []), accs)
    profile = ((accs[0] + accs[1]) + (accs[2] + accs[3])) * (1.0 / ANGLES)

    def share(ref, which, t):
        return pltpu.make_async_remote_copy(
            src_ref=ref.at[det],
            dst_ref=ref.at[det],
            send_sem=small_sem.at[which, 0],
            recv_sem=small_sem.at[which, 1],
            device_id=(proj, (det + t) % DET),
            device_id_type=MESH,
        )

    def shared(ref, which, count):
        others = pl.ds(0, count)
        return pltpu.make_async_remote_copy(
            src_ref=ref.at[others],
            dst_ref=ref.at[others],
            send_sem=small_sem.at[which, 0],
            recv_sem=small_sem.at[which, 1],
            device_id=(mate, det),
            device_id_type=MESH,
        )

    def arrange(start, stop):
        @pl.loop(start, stop)
        def _(i):
            for u in range(16):
                ordered_out[i * 16 + u] = y_v[places[i // 8, 16 * (i % 8) + u]]

    profs[det] = profile
    for t in (1, 3):
        share(profs, 0, t).start()
    low = jnp.where(sub < 2, zero, pltpu.roll(profile, 2, 0))
    high = jnp.where(sub >= 6, zero, pltpu.roll(profile, 6, 0))
    window = profile
    for o in range(1, RIM + 1):
        window = window + jnp.where(lane >= o, pltpu.roll(profile, o, 1), pltpu.roll(low, o, 1))
        window = window + jnp.where(
            lane < 128 - o, pltpu.roll(profile, 128 - o, 1), pltpu.roll(high, 128 - o, 1)
        )
    column = det * COLS_DEV + (sub // 2) * 128 + lane
    counted = jnp.minimum(column + RIM, COLS - 1) - jnp.maximum(column - RIM, 0) + 1
    counted = counted.astype(jnp.float32)
    inner = profile - window / counted

    def magnitude(i, accs):
        return tuple(
            accs[u] + jnp.abs(y_v[i * 16 + u] - inner) + jnp.abs(y_v[i * 16 + 8 + u] - inner)
            for u in range(8)
        )

    accs = lax.fori_loop(0, ANGLES // 16, magnitude, (zero,) * 8)
    total = ((accs[0] + accs[1]) + (accs[2] + accs[3])) + ((accs[4] + accs[5]) + (accs[6] + accs[7]))
    total = jnp.where(rim, zero, total)
    arrange(0, ARRANGED)
    shared(profs, 0, 2).wait_recv()
    before = pltpu.roll(profs[(det + DET - 1) % DET], 2, 0)
    after = pltpu.roll(profs[(det + 1) % DET], 6, 0)
    before = jnp.where((sub < 2) & (det > 0), before, zero)
    after = jnp.where((sub >= 6) & (det < DET - 1), after, zero)
    for o in range(1, RIM + 1):
        window = window + jnp.where(lane < o, pltpu.roll(before, o, 1), zero)
        window = window + jnp.where(lane >= 128 - o, pltpu.roll(after, 128 - o, 1), zero)
    delta = profile - window / counted
    delta_out[...] = delta

    outer = zero
    for m in range(FRAMES):
        outer = outer + pltpu.roll(jnp.where(rim, delta, zero), 2 * RIM * m, 1)

    def rim_magnitude(i, accs):
        return tuple(accs[u] + jnp.abs(edges[i * 8 + u] - outer) for u in range(8))

    accs = lax.fori_loop(0, PARTS * CHIPS // 8, rim_magnitude, (total,) + (zero,) * 7)
    total = ((accs[0] + accs[1]) + (accs[2] + accs[3])) + ((accs[4] + accs[5]) + (accs[6] + accs[7]))
    sums[det] = total
    for t in (2, 1, 3):
        share(sums, 1, t).start()
    arrange(ARRANGED, ANGLES // 16)
    shared(sums, 1, DET - 1).wait_recv()
    total = (sums[0] + sums[1]) + (sums[2] + sums[3])
    rows = jnp.broadcast_to(jnp.sum(total, axis=1, keepdims=True), (8, 128))
    rows = rows + pltpu.roll(rows, 4, 0)
    rows = rows + pltpu.roll(rows, 2, 0)
    scale = rows * (1.0 / (ANGLES * COLS)) + EPSILON
    bins = jnp.where(
        sub % 2 == 0,
        bin_counts[row_order[2 * proj]],
        bin_counts[row_order[2 * proj + 1]],
    ).astype(jnp.float32)
    factor_out[...] = bins / scale

    every = (pl.ds(0, PARTS), pl.ds(0, CHIPS - 1))
    pltpu.make_async_remote_copy(
        src_ref=own.at[every],
        dst_ref=recv.at[every],
        send_sem=send_sem.at[0],
        recv_sem=recv_sem.at[0],
        device_id=(mate, det),
        device_id_type=MESH,
    ).wait_send()
    shared(profs, 0, 2).wait_send()
    shared(sums, 1, DET - 1).wait_send()


BLOCK = 64
DEPTH = 16


def write_codes(ordered, delta, factor, out, block, sem):
    d, f = delta[...], factor[...]

    def copy(i):
        return pltpu.make_async_copy(
            block.at[i % DEPTH], out.at[pl.ds(i * BLOCK, BLOCK)], sem.at[i % DEPTH]
        )

    @pl.loop(0, ANGLES // BLOCK)
    def _(i):
        @pl.when(i >= DEPTH)
        def _():
            copy(i - DEPTH).wait()

        @pl.loop(0, BLOCK // 16)
        def _(k):
            for u in range(16):
                block[i % DEPTH, k * 16 + u] = (ordered[i * BLOCK + k * 16 + u] - d) * f

        copy(i).start()

    @pl.loop(ANGLES // BLOCK - DEPTH, ANGLES // BLOCK)
    def _(i):
        copy(i).wait()


def on_device(raw, slot_angle, segment_of, seg_owner, flat, dark, row_order, bin_counts):
    vmem = pl.BlockSpec(memory_space=pltpu.VMEM)
    hbm = pl.BlockSpec(memory_space=pltpu.HBM)
    dma = pltpu.SemaphoreType.DMA
    ordered, delta, factor = pl.pallas_call(
        exchange,
        name="exchange",
        out_shape=(
            jax.ShapeDtypeStruct((ANGLES, 8, 128), jnp.float32),
            jax.ShapeDtypeStruct((8, 128), jnp.float32),
            jax.ShapeDtypeStruct((8, 128), jnp.float32),
        ),
        in_specs=[hbm] * 8,
        out_specs=(vmem,) * 3,
        scratch_shapes=[
            pltpu.SMEM((CHIPS, 128), jnp.int32),
            pltpu.SMEM((SEGS,), jnp.int32),
            pltpu.SMEM((ROWS,), jnp.int32),
            pltpu.SMEM((ROWS,), jnp.int32),
            pltpu.VMEM((CHIPS, 128), jnp.int32),
            pltpu.VMEM((8, 128), jnp.int32),
            pltpu.SMEM((CHIPS, 128), jnp.int32),
            pltpu.VMEM((CHIPS, 128), jnp.int32),
            pltpu.SMEM((8, 128), jnp.int32),
            pltpu.VMEM((8, 128), jnp.int32),
            pltpu.VMEM((SLOTS, ROWS, COLS_DEV), jnp.bfloat16),
            pltpu.VMEM((PARTS, CHIPS, PAIRS, 16, 128), jnp.bfloat16),
            pltpu.VMEM((PARTS, CHIPS, PAIRS, 16, 128), jnp.bfloat16),
            pltpu.VMEM((PARTS, CHIPS, PAIRS, 16, 128), jnp.bfloat16),
            pltpu.VMEM((PARTS, CHIPS, PAIRS, 16, 128), jnp.bfloat16),
            pltpu.VMEM((ANGLES, 8, 128), jnp.float32),
            pltpu.VMEM((SEGS, ROWS, COLS_DEV), jnp.float32),
            pltpu.VMEM((SEGS, ROWS, COLS_DEV), jnp.float32),
            pltpu.VMEM((256, 256), jnp.float32),
            pltpu.VMEM((256, 256), jnp.bfloat16),
            pltpu.VMEM((HALVES, RING, RING, HSEGS, 16, 128), jnp.int16),
            pltpu.VMEM((HALVES, RING, RING, HSEGS, 16, 128), jnp.int16),
            pltpu.VMEM((HALVES, RING, RING, HSEGS, 16, 128), jnp.int16),
            pltpu.VMEM((HALVES, RING, RING, HSEGS, 16, 128), jnp.int16),
            pltpu.VMEM((HALVES, RING, HSEGS, 16, 128), jnp.int16),
            pltpu.VMEM((HALVES, RING, HSEGS, 16, 128), jnp.int16),
            pltpu.VMEM((PARTS * CHIPS, 8, 128), jnp.float32),
            pltpu.VMEM((SEGS, 8, 128), jnp.float32),
            pltpu.VMEM((SEGS, 8, 128), jnp.float32),
            pltpu.VMEM((DET, 8, 128), jnp.float32),
            pltpu.VMEM((DET, 8, 128), jnp.float32),
            dma((6,)),
            dma((PARTS,)),
            dma((2,)),
            dma((2,)),
            dma((1,)),
            dma((PARTS + 1,)),
            dma((1,)),
            dma((PARTS - 1 + len(LAST),)),
            dma((2,)),
            dma((HALVES, 2)),
            dma((HALVES, 2)),
            dma((2, 2)),
        ],
        compiler_params=pltpu.CompilerParams(
            collective_id=0, has_side_effects=True, vmem_limit_bytes=40 << 20
        ),
    )(
        *(
            pltpu.with_memory_space_constraint(a, pltpu.HBM)
            for a in (
                slot_angle.reshape(CHIPS, 2 * SLOTS),
                segment_of.reshape(8, 128),
                seg_owner,
                row_order,
                bin_counts,
                raw,
                flat,
                dark,
            )
        )
    )
    codes = pl.pallas_call(
        write_codes,
        name="write_codes",
        out_shape=jax.ShapeDtypeStruct((ANGLES, 8, 128), jnp.float32),
        in_specs=[vmem, vmem, vmem],
        out_specs=hbm,
        scratch_shapes=[pltpu.VMEM((DEPTH, BLOCK, 8, 128), jnp.float32), dma((DEPTH,))],
        compiler_params=pltpu.CompilerParams(vmem_limit_bytes=16 << 20),
    )(ordered, delta, factor)
    return codes.reshape(ANGLES, TILES, 2, 128).transpose(0, 2, 1, 3).reshape(ANGLES, 2, COLS_DEV)


def solution(mesh):
    return jax.shard_map(
        on_device,
        mesh=mesh,
        in_specs=(
            P("proj", None, "det"),
            P(),
            P(),
            P(),
            P("proj", None, "det"),
            P("proj", None, "det"),
            P(),
            P(),
        ),
        out_specs=P(None, "proj", "det"),
        check_vma=False,
    )
```
